128 devices in a mesh: sx: 8 (over y, z_hi), sy: 16 (over z_lo, x, core).
Axes of the slice: x: 4, y: 4, z: 4 (z_hi: 2, z_lo: 2; z = z_hi * 2 + z_lo), core: 2. Of those that a mesh axis runs over, the one named last changes fastest.
Arguments:
- quad_features: bfloat16 [8, 16, 16384, 64], P('sx', 'sy'), may hold values from -6 to 6
- w_first: bfloat16 [64, 512], replicated, may hold values from -0.75 to 0.75
- w_second: bfloat16 [512, 512], replicated, may hold values from -0.25 to 0.25
- w_third: bfloat16 [512, 128], replicated, may hold values from -0.25 to 0.25
- quad_block: int32 [8, 16, 16384], P('sx', 'sy'), may hold values from 0 to 255
- diag_tiles: float32 [64, 64, 16, 2048], P(None, None, 'sx', 'sy'), may hold values from -0.0078125 to 0.0078125
- x_tiles: float32 [64, 64, 16, 2048], P(None, None, 'sx', 'sy'), may hold values from -0.48125 to 0.03125
- y_tiles: float32 [64, 64, 16, 2048], P(None, None, 'sx', 'sy'), may hold values from -0.48125 to 0.03125
- p_tiles: float32 [64, 64, 16, 2048], P(None, None, 'sx', 'sy'), may hold values from -0.48125 to 0.03125
- tile_cols: int32 [8, 16, 256], P('sx', 'sy'), may hold values from 0 to 255, each once within a row
- x_map: int32 [8, 16, 128], P('sx', 'sy'), may hold values from 0 to 127, each once within a row
- y_map: int32 [8, 16, 2], P('sx', 'sy'), may hold values from 0 to 1, each once within a row
Outputs:
- adjoint: float32 [64, 16, 2048], P(None, 'sx', 'sy')
- residual: float32 [64, 16, 2048], P(None, 'sx', 'sy')
The draws below stay inside these ranges and needn't reach their ends.
Inputs may be any that keep to these rules, and one draw needn't show every extreme that they name: `quad_block`: each entry names a local block of the receiving subdomain. `tile_cols`: each subdomain's row is a permutation of its 256 local blocks. `x_map`: each subdomain's row is a permutation of 0 to 127. `y_map`: each subdomain's row is a permutation of 0 to 1.
All inputs are finite; a program needn't handle non-finite values.
Results may differ from the reference program's by a relative error of at most 0.0038.
Values may be sent and summed in bfloat16 or wider, within the bound.
A program may use at most 192 MiB of HBM per device.

```python
import jax
import jax.numpy as jnp
from jax import lax

BLOCK_DOFS = 64
FEATURES = 64
HIDDEN_UNITS = 512
BLOCKS_X = 2
BLOCKS_Y = 128
Q_DEV = 16384
ITERS = 3
SUBS_X = 8
SUBS_Y = 16
PER_BLOCK = 64
TOTAL_X = 16
TOTAL_Y = 2048
N_SX = 8
N_SY = 16


def coupling_draw(key, strength_lo, strength_hi):
    noise_key, strength_key = jax.random.split(key)
    shape = (BLOCK_DOFS, BLOCK_DOFS, TOTAL_X, TOTAL_Y)
    noise = jax.random.uniform(noise_key, shape, jnp.float32, -2.0 / BLOCK_DOFS, 2.0 / BLOCK_DOFS)
    strength = jax.random.uniform(strength_key, (BLOCK_DOFS, 1, TOTAL_X, TOTAL_Y), jnp.float32, strength_lo, strength_hi)
    identity = (jnp.arange(BLOCK_DOFS)[:, None] == jnp.arange(BLOCK_DOFS)[None, :]).astype(jnp.float32)[:, :, None, None]
    return noise - identity * strength


def draw_x_tiles(key, part):
    key = jax.random.fold_in(key, 11)
    return coupling_draw(key, 0.25, 0.45)


def draw_y_tiles(key, part):
    key = jax.random.fold_in(key, 12)
    return coupling_draw(key, 0.25, 0.45)


def draw_p_tiles(key, part):
    key = jax.random.fold_in(key, 13)
    return coupling_draw(key, 0.25, 0.45)


def touch_ends(values, stream_key, least, largest):
    dims = values.shape
    index_at = [jax.random.randint(jax.random.fold_in(stream_key, axis), (), 0, dims[axis]) for axis in range(len(dims))]
    values = values.at[tuple(index_at)].set(least)
    longest = dims.index(max(dims))
    index_at[longest] = (index_at[longest] + 1) % dims[longest]
    return values.at[tuple(index_at)].set(largest)


def steps_of(stream_key, extent, shards, least, largest):
    level = 1.0
    for dim, parts in shards:
        heights = jax.random.uniform(jax.random.fold_in(jax.random.fold_in(stream_key, 6), dim), (parts,), jnp.float32, least / len(shards), largest / len(shards))
        level = level * jnp.repeat(jnp.exp(heights), extent[dim] // parts).reshape((-1,) + (1,) * (len(extent) - 1 - dim))
    return level


def centred(own_key, extent, deviation, reach, cuts=(), kind=jnp.bfloat16):
    entries = deviation * jax.random.normal(own_key, extent, jnp.float32)
    if cuts:
        entries = entries * steps_of(own_key, extent, cuts, -0.22, 0.18)
    return jnp.clip(entries, -reach, reach).astype(kind)


def setup_inputs(seed: int = 0) -> dict:
    seeds = jax.random.split(jax.random.key(seed), 13)
    return {
        "quad_features": centred(seeds[0], (SUBS_X, SUBS_Y, Q_DEV, FEATURES), 1.0, 6.0, ((0, 8), (1, 16))),
        "w_first": centred(seeds[1], (FEATURES, HIDDEN_UNITS), FEATURES ** -0.5, 0.75),
        "w_second": centred(seeds[2], (HIDDEN_UNITS, HIDDEN_UNITS), HIDDEN_UNITS ** -0.5, 0.25),
        "w_third": centred(seeds[3], (HIDDEN_UNITS, 2 * BLOCK_DOFS), HIDDEN_UNITS ** -0.5, 0.25),
        "quad_block": touch_ends(jax.random.randint(seeds[4], (SUBS_X, SUBS_Y, Q_DEV), 0, BLOCKS_X * BLOCKS_Y), jax.random.fold_in(seeds[4], 1), 0, (BLOCKS_X * BLOCKS_Y) - 1).astype(jnp.int32),
        "diag_tiles": jnp.clip(jax.random.uniform(seeds[5], (BLOCK_DOFS, BLOCK_DOFS, TOTAL_X, TOTAL_Y), jnp.float32, -0.0078125, 0.0078125) * steps_of(seeds[5], (BLOCK_DOFS, BLOCK_DOFS, TOTAL_X, TOTAL_Y), ((2, 8), (3, 16)), -0.4, 0.0), -0.0078125, 0.0078125),
        "x_tiles": draw_x_tiles(jax.random.fold_in(seeds[12], 71), 0),
        "y_tiles": draw_y_tiles(jax.random.fold_in(seeds[12], 71), 0),
        "p_tiles": draw_p_tiles(jax.random.fold_in(seeds[12], 71), 0),
        "tile_cols": jax.vmap(lambda own: jax.random.permutation(own, BLOCKS_X * BLOCKS_Y))(jax.random.split(seeds[9], SUBS_X * SUBS_Y)).reshape((SUBS_X, SUBS_Y, BLOCKS_X * BLOCKS_Y)).astype(jnp.int32),
        "x_map": jax.vmap(lambda own: jax.random.permutation(own, BLOCKS_Y))(jax.random.split(seeds[10], SUBS_X * SUBS_Y)).reshape((SUBS_X, SUBS_Y, BLOCKS_Y)).astype(jnp.int32),
        "y_map": jax.vmap(lambda own: jax.random.permutation(own, BLOCKS_X))(jax.random.split(seeds[11], SUBS_X * SUBS_Y)).reshape((SUBS_X, SUBS_Y, BLOCKS_X)).astype(jnp.int32),
    }


HIGHEST = lax.Precision.HIGHEST
DIAG_SHIFT = 5.0


def apply_tiles(tile_set, vector):
    return jnp.einsum("ijab,jab->iab", tile_set, vector, precision=HIGHEST)


def apply_transposed(tile_set, vector):
    return jnp.einsum("jiab,jab->iab", tile_set, vector, precision=HIGHEST)


def constitutive(features, w_first, w_second, w_third):
    hidden_one = jax.nn.silu(jnp.dot(features, w_first, preferred_element_type=jnp.float32)).astype(jnp.bfloat16)
    hidden_two = jax.nn.silu(jnp.dot(hidden_one, w_second, preferred_element_type=jnp.float32)).astype(jnp.bfloat16)
    output = jnp.dot(hidden_two, w_third, preferred_element_type=jnp.float32)
    stress = output[:, :BLOCK_DOFS]
    tangent = jax.nn.softplus(output[:, BLOCK_DOFS:]) / PER_BLOCK
    return jnp.concatenate([stress, tangent], axis=1).astype(jnp.bfloat16)


def split_grid(vector):
    return vector.reshape(BLOCK_DOFS, N_SX, BLOCKS_X, N_SY, BLOCKS_Y)


def join_grid(grid_view):
    return grid_view.reshape(BLOCK_DOFS, TOTAL_X, TOTAL_Y)


def to_local(vector):
    return split_grid(vector).transpose(0, 1, 3, 2, 4).reshape(BLOCK_DOFS, N_SX, N_SY, BLOCKS_X * BLOCKS_Y)


def from_local(local_view):
    shaped = local_view.reshape(BLOCK_DOFS, N_SX, N_SY, BLOCKS_X, BLOCKS_Y)
    return shaped.transpose(0, 1, 3, 2, 4).reshape(BLOCK_DOFS, TOTAL_X, TOTAL_Y)


def take_along(source, index, axis):
    return jnp.take_along_axis(source, jnp.broadcast_to(index, source.shape).astype(jnp.int32), axis=axis)


def operate(vector, diagonal, sym_tiles, x_tiles, y_tiles, p_tiles, tile_cols, x_map, y_map):
    result = diagonal * vector + apply_tiles(sym_tiles, vector)
    grid_view = split_grid(vector)
    first_layer_x = grid_view[:, :, 0]
    next_layer_x = jnp.concatenate([first_layer_x[:, 1:], jnp.zeros_like(first_layer_x[:, :1])], axis=1)
    beyond_x = take_along(next_layer_x, x_map[None], 3)
    partner_x = jnp.concatenate([grid_view[:, :, 1:], beyond_x[:, :, None]], axis=2)
    result = result + apply_tiles(x_tiles, join_grid(partner_x))
    transposed_x = split_grid(apply_transposed(x_tiles, vector))
    outgoing_x = take_along(transposed_x[:, :, BLOCKS_X - 1], jnp.argsort(x_map, axis=-1)[None], 3)
    incoming_x = jnp.concatenate([jnp.zeros_like(outgoing_x[:, :1]), outgoing_x[:, :-1]], axis=1)
    result = result + join_grid(jnp.concatenate([incoming_x[:, :, None], transposed_x[:, :, :BLOCKS_X - 1]], axis=2))

    first_layer_y = grid_view[..., 0]
    next_layer_y = jnp.concatenate([first_layer_y[..., 1:], jnp.zeros_like(first_layer_y[..., :1])], axis=3)
    beyond_y = take_along(next_layer_y, y_map.transpose(0, 2, 1)[None], 2)
    partner_y = jnp.concatenate([grid_view[..., 1:], beyond_y[..., None]], axis=4)
    result = result + apply_tiles(y_tiles, join_grid(partner_y))
    transposed_y = split_grid(apply_transposed(y_tiles, vector))
    outgoing_y = take_along(transposed_y[..., BLOCKS_Y - 1], jnp.argsort(y_map, axis=-1).transpose(0, 2, 1)[None], 2)
    incoming_y = jnp.concatenate([jnp.zeros_like(outgoing_y[..., :1]), outgoing_y[..., :-1]], axis=3)
    result = result + join_grid(jnp.concatenate([incoming_y[..., None], transposed_y[..., :BLOCKS_Y - 1]], axis=4))

    gathered = take_along(to_local(vector), tile_cols[None], 3)
    result = result + apply_tiles(p_tiles, from_local(gathered))
    transposed_p = to_local(apply_transposed(p_tiles, vector))
    result = result + from_local(take_along(transposed_p, jnp.argsort(tile_cols, axis=-1)[None], 3))
    return result


def reference(quad_features, w_first, w_second, w_third, quad_block, diag_tiles, x_tiles, y_tiles, p_tiles, tile_cols, x_map, y_map):
    senders = N_SX * N_SY
    blocks = BLOCKS_X * BLOCKS_Y
    row_width = 2 * BLOCK_DOFS
    slot_count = Q_DEV // senders
    features_all = quad_features.reshape(senders, Q_DEV, FEATURES)
    produced = lax.map(lambda sender_rows: constitutive(sender_rows, w_first, w_second, w_third), features_all)
    received = produced.reshape(senders, senders, slot_count, row_width).transpose(1, 0, 2, 3).reshape(senders, Q_DEV, row_width)
    owners = quad_block.reshape(senders, Q_DEV)

    def assemble(pair):
        received_rows, owner_block = pair
        onehot = (owner_block[None, :] == jnp.arange(blocks, dtype=jnp.int32)[:, None]).astype(jnp.bfloat16)
        return jnp.dot(onehot, received_rows, preferred_element_type=jnp.float32)

    assembled = lax.map(assemble, (received, owners))
    fields = assembled.reshape(N_SX, N_SY, BLOCKS_X, BLOCKS_Y, row_width).transpose(4, 0, 2, 1, 3).reshape(row_width, TOTAL_X, TOTAL_Y)
    load_vector = fields[:BLOCK_DOFS]
    tangent_sum = fields[BLOCK_DOFS:]
    diagonal = DIAG_SHIFT + tangent_sum
    sym_tiles = diag_tiles + diag_tiles.transpose(1, 0, 2, 3)
    jacobi = diagonal + 2.0 * jnp.moveaxis(jnp.diagonal(diag_tiles, axis1=0, axis2=1), -1, 0)

    adjoint = jnp.zeros_like(load_vector)
    residual = load_vector
    precond = residual / jacobi
    direction = precond
    rho_now = jnp.sum(residual * precond)
    for sweep in range(ITERS):
        applied = operate(direction, diagonal, sym_tiles, x_tiles, y_tiles, p_tiles, tile_cols, x_map, y_map)
        step_size = rho_now / jnp.sum(direction * applied)
        adjoint = adjoint + step_size * direction
        residual = residual - step_size * applied
        precond = residual / jacobi
        rho_next = jnp.sum(residual * precond)
        direction = precond + (rho_next / rho_now) * direction
        rho_now = rho_next
    return adjoint, residual
```

```python
import functools

import jax
import jax.numpy as jnp
from jax import lax
from jax.experimental import pallas as pl
from jax.experimental.pallas import tpu as pltpu
from jax.sharding import PartitionSpec as P

BLOCK_DOFS = 64
FEATURES = 64
ITERS = 3
PER_BLOCK = 64
DIAG_SHIFT = 5.0
MESH = pl.DeviceIdType.MESH
F32 = jnp.float32
BF16 = jnp.bfloat16
EVEN = pl.ds(0, 64, stride=2)
ODD = pl.ds(1, 64, stride=2)


def constitutive(features, w_first, w_second, w_third):
    hidden_one = jax.nn.silu(jnp.dot(features, w_first, preferred_element_type=F32)).astype(BF16)
    hidden_two = jax.nn.silu(jnp.dot(hidden_one, w_second, preferred_element_type=F32)).astype(BF16)
    output = jnp.dot(hidden_two, w_third, preferred_element_type=F32)
    stress = output[:, :BLOCK_DOFS]
    tangent = jax.nn.softplus(output[:, BLOCK_DOFS:]) / PER_BLOCK
    return jnp.concatenate([stress, tangent], axis=1).astype(BF16)


def permute(value, matrix, transposed):
    rows = value.shape[0]
    high = value.astype(BF16)
    rest = value - high.astype(F32)
    middle = rest.astype(BF16)
    low = (rest - middle.astype(F32)).astype(BF16)
    parts = jnp.concatenate([high, middle, low], axis=0)
    dims = (((1,), (1 if transposed else 0,)), ((), ()))
    product = lax.dot_general(parts, matrix, dims, preferred_element_type=F32)
    return product[:rows] + product[rows : 2 * rows] + product[2 * rows :]


def swap_pairs(row, swap):
    lane = lax.broadcasted_iota(jnp.int32, row.shape, 1)
    swapped = jnp.where(lane % 2 == 0, pltpu.roll(row, 127, 1), pltpu.roll(row, 1, 1))
    return jnp.where(swap > 0, swapped, row)


def column(row):
    return jnp.broadcast_to(row[0:1], (128, 128)).T


def cg_kernel(
    n_sx,
    n_sy,
    rows_hbm,
    owner_ref,
    diag_hbm,
    x_hbm,
    y_hbm,
    p_hbm,
    cols_ref,
    xmap_ref,
    yswap_ref,
    adjoint_ref,
    residual_ref,
    rows_ref,
    e_ref,
    x_ref,
    y_ref,
    p_ref,
    mp_ref,
    mx_ref,
    diag_ref,
    jac_ref,
    z_ref,
    d_ref,
    s_ref,
    vb_ref,
    red_ref,
    acc_ref,
    tmp_ref,
    part_p_ref,
    hx_out,
    hy_out,
    ix_out,
    iy_out,
    hx_in,
    hy_in,
    ix_in,
    iy_in,
    sum_y,
    sum_x,
    local_sem,
    halo_send,
    halo_recv,
    sum_send,
    sum_recv,
):
    i = lax.axis_index("sx")
    j = lax.axis_index("sy")
    loads = [
        pltpu.make_async_copy(src, dst, local_sem.at[k])
        for k, (src, dst) in enumerate(
            [(rows_hbm, rows_ref), (diag_hbm, e_ref), (x_hbm, x_ref), (y_hbm, y_ref), (p_hbm, p_ref)]
        )
    ]
    for load in loads:
        load.start()
    barrier = pltpu.get_barrier_semaphore()
    for k in range(1, n_sx):
        pl.semaphore_signal(barrier, inc=1, device_id=(lax.rem(i + k, n_sx), j), device_id_type=MESH)
    for k in range(1, n_sy):
        pl.semaphore_signal(barrier, inc=1, device_id=(i, lax.rem(j + k, n_sy)), device_id_type=MESH)
    pl.semaphore_wait(barrier, n_sx + n_sy - 2)

    def send(src, dst, slot, to):
        copy = pltpu.make_async_remote_copy(
            src_ref=src,
            dst_ref=dst,
            send_sem=halo_send.at[slot],
            recv_sem=halo_recv.at[slot],
            device_id=to,
            device_id_type=MESH,
        )
        copy.start()
        return copy

    x_next, x_prev = (lax.rem(i + 1, n_sx), j), (lax.rem(i + n_sx - 1, n_sx), j)
    y_next, y_prev = (i, lax.rem(j + 1, n_sy)), (i, lax.rem(j + n_sy - 1, n_sy))

    mp_ref[...] = (lax.broadcasted_iota(jnp.int32, (256, 256), 0) == cols_ref[0:1]).astype(F32).astype(BF16)
    mx_ref[...] = (lax.broadcasted_iota(jnp.int32, (128, 128), 0) == xmap_ref[0:1]).astype(F32).astype(BF16)
    yswap = yswap_ref[...]

    loads[0].wait()

    def assemble(step, total):
        owners = owner_ref[pl.ds(pl.multiple_of(step * 8, 8), 8), :]
        block = lax.broadcasted_iota(jnp.int32, (256, 128), 0)
        onehot = jnp.concatenate(
            [(block == owners[e : e + 1]).astype(F32).astype(BF16) for e in range(8)], axis=1
        )
        rows = rows_ref[pl.ds(pl.multiple_of(step * 1024, 1024), 1024), :]
        return total + jnp.dot(onehot, rows, preferred_element_type=F32)

    fields = lax.fori_loop(0, 16, assemble, jnp.zeros((256, 128), F32)).T
    residual_ref[EVEN, :] = fields[:64, :128]
    residual_ref[ODD, :] = fields[:64, 128:]
    diag_ref[EVEN, :] = fields[64:, :128] + DIAG_SHIFT
    diag_ref[ODD, :] = fields[64:, 128:] + DIAG_SHIFT
    for load in loads[1:]:
        load.wait()
    for k in range(64):
        jac_ref[2 * k : 2 * k + 2, :] = e_ref[k, 2 * k : 2 * k + 2, :]
    jac_ref[...] = diag_ref[...] + 2.0 * jac_ref[...]

    def transposed_pass(tiles):
        def body(step, total):
            for u in range(2):
                k = step * 2 + u
                total = total + tiles[k].reshape(16, 8, 128) * vb_ref[k][None]
            return total

        return lax.fori_loop(0, 32, body, jnp.zeros((16, 8, 128), F32)).reshape(128, 128)

    def forward_pass(tiles, partner):
        partner = partner.reshape(16, 8, 128)

        def body(step, carry):
            for u in range(2):
                k = step * 2 + u
                red_ref[k] += jnp.sum(tiles[k].reshape(16, 8, 128) * partner, axis=0)
            return carry

        lax.fori_loop(0, 32, body, 0)

    def both_pass(tiles, partner, first):
        partner = partner.reshape(16, 8, 128)

        def body(step, total):
            for u in range(2):
                k = step * 2 + u
                tile = tiles[k].reshape(16, 8, 128)
                forward = jnp.sum(tile * partner, axis=0)
                red_ref[k] = forward if first else red_ref[k] + forward
                total = total + tile * vb_ref[k][None]
            return total

        return lax.fori_loop(0, 32, body, jnp.zeros((16, 8, 128), F32)).reshape(128, 128)

    def global_sum(it):
        copies = []
        for stage, (buffer, mine, count) in enumerate([(sum_y, j, n_sy), (sum_x, i, n_sx)]):
            for k in range(1, count):
                peer = lax.rem(mine + k, count)
                copy = pltpu.make_async_remote_copy(
                    src_ref=buffer.at[it, mine],
                    dst_ref=buffer.at[it, mine],
                    send_sem=sum_send.at[it, stage],
                    recv_sem=sum_recv.at[it, stage],
                    device_id=(i, peer) if stage == 0 else (peer, j),
                    device_id_type=MESH,
                )
                copy.start()
            others = pltpu.make_async_copy(
                buffer.at[it, pl.ds(0, count - 1)], buffer.at[it, pl.ds(0, count - 1)], sum_recv.at[it, stage]
            )
            others.wait()
            total = jnp.sum(buffer[it], axis=0)
            if stage == 0:
                sum_x[it, i] = total
            copies.append((buffer, count, it, stage))
        return jnp.sum(total, axis=1, keepdims=True), copies

    lane = lax.broadcasted_iota(jnp.int32, (128, 128), 1)
    edge_x = jnp.where(i == n_sx - 1, 0.0, 1.0)
    edge_y = jnp.where(j == n_sy - 1, 0.0, 1.0)
    start_x = jnp.where(i == 0, 0.0, 1.0)
    start_y = jnp.where(j == 0, 0.0, 1.0)
    sent = []
    summed = []
    alpha = gamma_old = None
    for it in range(ITERS):
        residual = residual_ref[...]
        z = residual / jac_ref[...]
        z_ref[...] = z
        z_even, z_odd = z_ref[EVEN, :], z_ref[ODD, :]
        hx_out[it] = z_even
        hx = send(hx_out.at[it], hx_in.at[it], 4 * it, x_prev)
        hy_out[it] = z.T[0:8]
        hy = send(hy_out.at[it], hy_in.at[it], 4 * it + 1, y_prev)
        for q in range(4):
            vb_ref[:, 2 * q, :] = z_even
            vb_ref[:, 2 * q + 1, :] = z_odd
        tmp_ref[...] = transposed_pass(x_ref)
        ix_out[it] = permute(tmp_ref[ODD, :], mx_ref[...], True)
        ix = send(ix_out.at[it], ix_in.at[it], 4 * it + 2, x_next)
        turned = transposed_pass(y_ref)
        iy_out[it] = swap_pairs(turned.T[120:128], yswap)
        iy = send(iy_out.at[it], iy_in.at[it], 4 * it + 3, y_next)
        acc_ref[...] = diag_ref[...] * z + jnp.where(lane == 0, 0.0, pltpu.roll(turned, 1, 1))
        acc_ref[ODD, :] += tmp_ref[EVEN, :]
        acc_ref[...] += both_pass(e_ref, z, True)
        flat = permute(jnp.concatenate([z_even, z_odd], axis=1), mp_ref[...], False)
        part_p_ref[EVEN, :] = flat[:, :128]
        part_p_ref[ODD, :] = flat[:, 128:]
        tmp_ref[...] = both_pass(p_ref, part_p_ref[...], False)
        flat = permute(jnp.concatenate([tmp_ref[EVEN, :], tmp_ref[ODD, :]], axis=1), mp_ref[...], True)
        acc_ref[EVEN, :] += flat[:, :128]
        acc_ref[ODD, :] += flat[:, 128:]
        hx.wait_recv()
        tmp_ref[EVEN, :] = z_odd
        tmp_ref[ODD, :] = permute(hx_in[it], mx_ref[...], False) * edge_x
        forward_pass(x_ref, tmp_ref[...])
        hy.wait_recv()
        beyond = column(swap_pairs(hy_in[it], yswap)) * edge_y
        forward_pass(y_ref, jnp.where(lane == 127, beyond, pltpu.roll(z, 127, 1)))
        for a, part in ((0, EVEN), (1, ODD)):
            total = red_ref[:, a, :]
            for q in range(1, 4):
                total = total + red_ref[:, 2 * q + a, :]
            acc_ref[part, :] += total
        ix.wait_recv()
        acc_ref[EVEN, :] += ix_in[it] * start_x
        iy.wait_recv()
        acc_ref[...] += jnp.where(lane == 0, column(iy_in[it, 7:8]) * start_y, 0.0)
        sent += [hx, hy, ix, iy]
        applied = acc_ref[...]
        sums = jnp.concatenate(
            [
                jnp.sum(residual * z, axis=0, keepdims=True),
                jnp.sum(z * applied, axis=0, keepdims=True),
                jnp.zeros((6, 128), F32),
            ],
            axis=0,
        )
        sum_y[it, j] = sums
        totals, copies = global_sum(it)
        summed += copies
        gamma, delta = totals[0:1], totals[1:2]
        if it == 0:
            alpha = gamma / delta
            direction, image = z, applied
            adjoint_ref[...] = alpha * direction
        else:
            beta = gamma / gamma_old
            alpha = gamma / (delta - beta * gamma / alpha)
            direction = z + beta * d_ref[...]
            image = applied + beta * s_ref[...]
            adjoint_ref[...] += alpha * direction
        gamma_old = gamma
        residual_ref[...] = residual - alpha * image
        if it + 1 < ITERS:
            d_ref[...] = direction
            s_ref[...] = image
    for copy in sent:
        copy.wait_send()
    for buffer, count, it, stage in summed:
        pltpu.make_async_copy(
            buffer.at[it, pl.ds(0, count - 1)], buffer.at[it, pl.ds(0, count - 1)], sum_send.at[it, stage]
        ).wait()


def local(n_sx, n_sy, *args):
    (
        quad_features,
        w_first,
        w_second,
        w_third,
        quad_block,
        diag_tiles,
        x_tiles,
        y_tiles,
        p_tiles,
        tile_cols,
        x_map,
        y_map,
    ) = args
    sample_count = quad_features.shape[2]
    devices = n_sx * n_sy
    slots = sample_count // devices
    features = quad_features.reshape(sample_count, FEATURES)
    produced = constitutive(features, w_first, w_second, w_third).reshape(devices, slots, 2 * BLOCK_DOFS)
    received = lax.all_to_all(produced, ("sx", "sy"), split_axis=0, concat_axis=0, tiled=True)
    received = received.reshape(sample_count, 2 * BLOCK_DOFS)
    tiles = [t.reshape(64, 128, 128) for t in (diag_tiles, x_tiles, y_tiles, p_tiles)]
    owners = quad_block.reshape(128, 128)
    cols = jnp.broadcast_to(tile_cols.reshape(1, 256), (8, 256))
    xmap = jnp.broadcast_to(x_map.reshape(1, 128), (8, 128))
    yswap = jnp.broadcast_to(y_map[0, 0, 0], (8, 128))
    hbm = pl.BlockSpec(memory_space=pl.ANY)
    vmem = pl.BlockSpec(memory_space=pltpu.VMEM)
    square = pltpu.VMEM((128, 128), F32)
    adjoint, residual = pl.pallas_call(
        functools.partial(cg_kernel, n_sx, n_sy),
        out_shape=[jax.ShapeDtypeStruct((128, 128), F32)] * 2,
        in_specs=[hbm, vmem, hbm, hbm, hbm, hbm, vmem, vmem, vmem],
        out_specs=[vmem, vmem],
        scratch_shapes=[
            pltpu.VMEM((16384, 128), BF16),
            pltpu.VMEM((64, 128, 128), F32),
            pltpu.VMEM((64, 128, 128), F32),
            pltpu.VMEM((64, 128, 128), F32),
            pltpu.VMEM((64, 128, 128), F32),
            pltpu.VMEM((256, 256), BF16),
            pltpu.VMEM((128, 128), BF16),
            square,
            square,
            square,
            square,
            square,
            pltpu.VMEM((64, 8, 128), F32),
            pltpu.VMEM((64, 8, 128), F32),
            square,
            square,
            square,
            pltpu.VMEM((ITERS, 64, 128), F32),
            pltpu.VMEM((ITERS, 8, 128), F32),
            pltpu.VMEM((ITERS, 64, 128), F32),
            pltpu.VMEM((ITERS, 8, 128), F32),
            pltpu.VMEM((ITERS, 64, 128), F32),
            pltpu.VMEM((ITERS, 8, 128), F32),
            pltpu.VMEM((ITERS, 64, 128), F32),
            pltpu.VMEM((ITERS, 8, 128), F32),
            pltpu.VMEM((ITERS, n_sy, 8, 128), F32),
            pltpu.VMEM((ITERS, n_sx, 8, 128), F32),
            pltpu.SemaphoreType.DMA((5,)),
            pltpu.SemaphoreType.DMA((4 * ITERS,)),
            pltpu.SemaphoreType.DMA((4 * ITERS,)),
            pltpu.SemaphoreType.DMA((ITERS, 2)),
            pltpu.SemaphoreType.DMA((ITERS, 2)),
        ],
        compiler_params=pltpu.CompilerParams(
            collective_id=0, has_side_effects=True, vmem_limit_bytes=48 * 2**20
        ),
    )(received, owners, *tiles, cols, xmap, yswap)
    return adjoint.reshape(64, 2, 128), residual.reshape(64, 2, 128)


def solution(mesh):
    in_specs = (
        P("sx", "sy", None, None),
        P(),
        P(),
        P(),
        P("sx", "sy", None),
        P(None, None, "sx", "sy"),
        P(None, None, "sx", "sy"),
        P(None, None, "sx", "sy"),
        P(None, None, "sx", "sy"),
        P("sx", "sy", None),
        P("sx", "sy", None),
        P("sx", "sy", None),
    )
    out_specs = (P(None, "sx", "sy"), P(None, "sx", "sy"))
    return jax.shard_map(
        functools.partial(local, mesh.shape["sx"], mesh.shape["sy"]),
        mesh=mesh,
        in_specs=in_specs,
        out_specs=out_specs,
        check_vma=False,
    )
```

```python
import functools

import jax
import jax.numpy as jnp
from jax import lax
from jax.experimental import pallas as pl
from jax.experimental.pallas import tpu as pltpu
from jax.sharding import PartitionSpec as P

FEATURES = 64
ITERS = 3
PER_BLOCK = 64
DIAG_SHIFT = 5.0
MESH = pl.DeviceIdType.MESH
F32 = jnp.float32
BF16 = jnp.bfloat16
EVEN = pl.ds(0, 64, stride=2)
ODD = pl.ds(1, 64, stride=2)


def permute(value, matrix, transposed):
    rows = value.shape[0]
    high = value.astype(BF16)
    rest = value - high.astype(F32)
    middle = rest.astype(BF16)
    low = (rest - middle.astype(F32)).astype(BF16)
    parts = jnp.concatenate([high, middle, low], axis=0)
    dims = (((1,), (1 if transposed else 0,)), ((), ()))
    product = lax.dot_general(parts, matrix, dims, preferred_element_type=F32)
    return product[:rows] + product[rows : 2 * rows] + product[2 * rows :]


def swap_pairs(row, swap):
    lane = lax.broadcasted_iota(jnp.int32, row.shape, 1)
    swapped = jnp.where(lane % 2 == 0, pltpu.roll(row, 127, 1), pltpu.roll(row, 1, 1))
    return jnp.where(swap > 0, swapped, row)


def column(row):
    return jnp.broadcast_to(row, (128, 128)).T


def silu_of_half(u):
    return (u + u * jnp.tanh(u)).astype(BF16)


def kernel(
    feat_hbm,
    w1_ref,
    w2_ref,
    w3_ref,
    owner_ref,
    diag_hbm,
    x_hbm,
    y_hbm,
    p_hbm,
    cols_ref,
    xmap_ref,
    yswap_ref,
    adjoint_ref,
    residual_ref,
    feat_ref,
    w1h_ref,
    w2h_ref,
    prod_ref,
    ring_ref,
    plane_out,
    plane_ref,
    index_out,
    index_ref,
    e_ref,
    x_ref,
    y_ref,
    p_ref,
    mp_ref,
    mx_ref,
    vectors,
    vb_ref,
    red_ref,
    acc_ref,
    tmp_ref,
    hx_out,
    hy_out,
    ix_out,
    iy_out,
    hx_in,
    hy_in,
    ix_in,
    iy_in,
    sum_a,
    sum_b,
    local_sem,
    ring_send,
    ring_recv,
    plane_sem,
    index_sem,
    halo_send,
    halo_recv,
    sum_send,
    sum_recv,
):
    i = lax.axis_index("sx")
    j = lax.axis_index("sy")
    y, zh = i // 2, lax.rem(i, 2)
    zl, jl = j // 8, lax.rem(j, 8)
    x, core = jl // 2, lax.rem(j, 2)

    loads = [
        pltpu.make_async_copy(src, dst, local_sem.at[k])
        for k, (src, dst) in enumerate(
            [(feat_hbm, feat_ref), (diag_hbm, e_ref), (x_hbm, x_ref), (y_hbm, y_ref), (p_hbm, p_ref)]
        )
    ]
    for load in loads:
        load.start()

    def pick(first, second):
        return first * (1 - core) + second * core

    others = [(i, lax.rem(j + k, 16)) for k in range(1, 16)]
    others += [(lax.rem(i + k, 8), j) for k in range(1, 8)]
    others += [(lax.rem(i + k, 8), lax.rem(j + 8, 16)) for k in range(1, 8)]
    others += [(lax.rem(y + k, 4) * 2 + zh, j + 1 - 2 * core) for k in range(1, 4)]
    others += [(y * 2 + 1 - zh, lax.rem(j + 2 * k, 16)) for k in range(1, 8)]
    barrier = pltpu.get_barrier_semaphore()
    for other in others:
        pl.semaphore_signal(barrier, inc=1, device_id=other, device_id_type=MESH)

    w1h_ref[...] = (w1_ref[...].astype(F32) * 0.5).astype(BF16)
    w2h_ref[...] = (w2_ref[...].astype(F32) * 0.5).astype(BF16)

    place = pick(i * 2 + zl, zh * 8 + zl * 4 + x)

    def plane_device(t):
        return pick(t // 2, y * 2 + t // 8), pick(lax.rem(t, 2) * 8 + x * 2, lax.rem(t, 8) * 2 + 1)

    for t in range(16):
        for q in range(4):
            first = pick((t // 2) * 16 + (t % 2) * 8 + q * 2, (q * 2 + t // 8) * 16 + (t % 8) * 2)
            index_out[t, 2 * q : 2 * q + 2, :] = owner_ref[pl.ds(first, 2), :]
    index_ref[place] = index_out[place]
    pl.semaphore_wait(barrier, len(others))

    def send_index(s, carry):
        t = lax.rem(place + s, 16)
        pltpu.make_async_remote_copy(
            src_ref=index_out.at[t],
            dst_ref=index_ref.at[place],
            send_sem=index_sem.at[0],
            recv_sem=index_sem.at[1],
            device_id=plane_device(t),
            device_id_type=MESH,
        ).start()
        return carry

    lax.fori_loop(1, 16, send_index, 0)

    mp_ref[...] = (lax.broadcasted_iota(jnp.int32, (256, 256), 0) == cols_ref[0:1]).astype(F32).astype(BF16)
    mx_ref[...] = (lax.broadcasted_iota(jnp.int32, (128, 128), 0) == xmap_ref[0:1]).astype(F32).astype(BF16)
    yswap = yswap_ref[...]

    loads[0].wait()
    lane512 = lax.broadcasted_iota(jnp.int32, (256, 128), 1)

    def chunk(c, carry):
        k, part = c // 4, lax.rem(c, 4)
        pair = k // 2
        turn = jnp.where(k >= 6, 0, jnp.where(pair == 2, 2, 1 + 2 * pair))
        other_class = jnp.where(k >= 6, 7 - k, lax.rem(k, 2))
        dcore = lax.rem(core + other_class, 2)
        dx = lax.rem(x + turn * (1 - dcore), 4)
        dy = lax.rem(y + turn * dcore, 4)
        for half in range(2):
            blocks = []
            for u in range(2):
                t = part * 4 + half * 2 + u
                ri = (1 - dcore) * (t // 2) + dcore * (dy * 2 + t // 8)
                rj = (1 - dcore) * (lax.rem(t, 2) * 8 + dx * 2) + dcore * (lax.rem(t, 8) * 2 + 1)
                start = pl.multiple_of((ri * 16 + rj) * 128, 128)
                blocks.append(feat_ref[pl.ds(start, 128), :])
            rows = jnp.concatenate(blocks, axis=0)
            hidden = silu_of_half(jnp.dot(rows, w1h_ref[...], preferred_element_type=F32))
            hidden = silu_of_half(jnp.dot(hidden, w2h_ref[...], preferred_element_type=F32))
            output = jnp.dot(hidden, w3_ref[...], preferred_element_type=F32)
            softplus = jnp.maximum(output, 0.0) + jnp.log(1.0 + jnp.exp(-jnp.abs(output)))
            output = jnp.where(lane512 < 64, output, softplus * (1.0 / PER_BLOCK)).astype(BF16)
            prod_ref[c, 2 * half : 2 * half + 2] = output.reshape(2, 128, 128)
        slot = (1 - dcore) * (x * 2 + core) + dcore * (y * 2 + core)

        @pl.when(k < 7)
        def _():
            pltpu.make_async_remote_copy(
                src_ref=prod_ref.at[c],
                dst_ref=ring_ref.at[slot, pl.ds(part * 4, 4)],
                send_sem=ring_send,
                recv_sem=ring_recv.at[slot],
                device_id=(dy * 2 + zh, (zl * 4 + dx) * 2 + dcore),
                device_id_type=MESH,
            ).start()

        @pl.when(k == 7)
        def _():
            ring_ref[slot, pl.ds(part * 4, 4)] = prod_ref[c]

        return carry

    lax.fori_loop(0, 32, chunk, 0)

    mine = pick(x * 2 + core, y * 2 + core)
    pltpu.make_async_copy(index_ref.at[pl.ds(0, 15)], index_ref.at[pl.ds(0, 15)], index_sem.at[1]).wait()
    for s in range(1, 8):
        slot = lax.rem(mine + s, 8)
        pltpu.make_async_copy(ring_ref.at[slot], ring_ref.at[slot], ring_recv.at[slot]).wait()

    def reduce_rows(s, carry):
        t = lax.rem(place + s, 16)
        owners = index_ref[t]
        block = lax.broadcasted_iota(jnp.int32, (256, 128), 0)
        onehot = jnp.concatenate(
            [(block == owners[e : e + 1]).astype(F32).astype(BF16) for e in range(8)], axis=1
        )
        rows = ring_ref[:, t].reshape(1024, 128)
        plane_out[t] = jnp.dot(onehot, rows, preferred_element_type=F32).astype(BF16)

        @pl.when(s < 16)
        def _():
            pltpu.make_async_remote_copy(
                src_ref=plane_out.at[t],
                dst_ref=plane_ref.at[place],
                send_sem=plane_sem.at[0],
                recv_sem=plane_sem.at[1],
                device_id=plane_device(t),
                device_id_type=MESH,
            ).start()

        @pl.when(s == 16)
        def _():
            plane_ref[place] = plane_out[t]

        return carry

    lax.fori_loop(1, 17, reduce_rows, 0)
    for load in loads[1:]:
        load.wait()
    jac_ref, diag_ref, u_ref, w_ref, d_ref, s_ref, q_ref, zz_ref = (vectors.at[k] for k in range(8))
    for k in range(64):
        jac_ref[2 * k : 2 * k + 2, :] = e_ref[k, 2 * k : 2 * k + 2, :]
    pltpu.make_async_copy(plane_ref.at[pl.ds(0, 15)], plane_ref.at[pl.ds(0, 15)], plane_sem.at[1]).wait()
    total = plane_ref[0].astype(F32)
    for t in range(1, 16):
        total = total + plane_ref[t].astype(F32)
    fields = total.T
    residual_ref[EVEN, :] = fields[:64, :128]
    residual_ref[ODD, :] = fields[:64, 128:]
    diag_ref[EVEN, :] = fields[64:, :128] + DIAG_SHIFT
    diag_ref[ODD, :] = fields[64:, 128:] + DIAG_SHIFT
    jac_ref[...] = diag_ref[...] + 2.0 * jac_ref[...]

    x_next, x_prev = (lax.rem(i + 1, 8), j), (lax.rem(i + 7, 8), j)
    y_next, y_prev = (i, lax.rem(j + 1, 16)), (i, lax.rem(j + 15, 16))
    lane = lax.broadcasted_iota(jnp.int32, (128, 128), 1)
    edge_x = jnp.where(i == 7, 0.0, 1.0)
    edge_y = jnp.where(j == 15, 0.0, 1.0)
    start_x = jnp.where(i == 0, 0.0, 1.0)
    start_y = jnp.where(j == 0, 0.0, 1.0)

    def send(src, dst, slot, to):
        copy = pltpu.make_async_remote_copy(
            src_ref=src,
            dst_ref=dst,
            send_sem=halo_send.at[slot],
            recv_sem=halo_recv.at[slot],
            device_id=to,
            device_id_type=MESH,
        )
        copy.start()
        return copy

    def transposed_pass(tiles):
        def body(step, total):
            for u in range(2):
                k = step * 2 + u
                total = total + tiles[k].reshape(16, 8, 128) * vb_ref[k][None]
            return total

        return lax.fori_loop(0, 32, body, jnp.zeros((16, 8, 128), F32)).reshape(128, 128)

    def forward_pass(tiles, partner):
        partner = partner.reshape(16, 8, 128)

        def body(step, carry):
            for u in range(2):
                k = step * 2 + u
                red_ref[k] += jnp.sum(tiles[k].reshape(16, 8, 128) * partner, axis=0)
            return carry

        lax.fori_loop(0, 32, body, 0)

    def both_pass(tiles, partner, first):
        partner = partner.reshape(16, 8, 128)

        def body(step, total):
            for u in range(2):
                k = step * 2 + u
                tile = tiles[k].reshape(16, 8, 128)
                forward = jnp.sum(tile * partner, axis=0)
                red_ref[k] = forward if first else red_ref[k] + forward
                total = total + tile * vb_ref[k][None]
            return total

        return lax.fori_loop(0, 32, body, jnp.zeros((16, 8, 128), F32)).reshape(128, 128)

    index_b = i * 2 + zl

    def sum_begin(it, first, second):
        sum_a[it, jl] = jnp.concatenate(
            [jnp.sum(first, axis=0, keepdims=True), jnp.sum(second, axis=0, keepdims=True)], axis=0
        )
        for k in range(1, 8):
            pltpu.make_async_remote_copy(
                src_ref=sum_a.at[it, jl],
                dst_ref=sum_a.at[it, jl],
                send_sem=sum_send.at[it, 0],
                recv_sem=sum_recv.at[it, 0],
                device_id=(i, zl * 8 + lax.rem(jl + k, 8)),
                device_id_type=MESH,
            ).start()

    def sum_middle(it):
        pltpu.make_async_copy(sum_a.at[it, pl.ds(0, 7)], sum_a.at[it, pl.ds(0, 7)], sum_recv.at[it, 0]).wait()
        sum_b[it, index_b] = jnp.sum(sum_a[it], axis=0)
        for k in range(1, 16):
            peer = lax.rem(index_b + k, 16)
            pltpu.make_async_remote_copy(
                src_ref=sum_b.at[it, index_b],
                dst_ref=sum_b.at[it, index_b],
                send_sem=sum_send.at[it, 1],
                recv_sem=sum_recv.at[it, 1],
                device_id=(peer // 2, lax.rem(peer, 2) * 8 + jl),
                device_id_type=MESH,
            ).start()

    def sum_end(it):
        pltpu.make_async_copy(sum_b.at[it, pl.ds(0, 15)], sum_b.at[it, pl.ds(0, 15)], sum_recv.at[it, 1]).wait()
        total = jnp.sum(jnp.sum(sum_b[it], axis=0), axis=1, keepdims=True)
        return total[0:1], total[1:2]

    sent = []

    def apply(it, z, between):
        tmp_ref[...] = z
        z_even, z_odd = tmp_ref[EVEN, :], tmp_ref[ODD, :]
        hx_out[it] = z_even
        hx = send(hx_out.at[it], hx_in.at[it], 4 * it, x_prev)
        hy_out[it] = z.T[0:8]
        hy = send(hy_out.at[it], hy_in.at[it], 4 * it + 1, y_prev)
        for q in range(4):
            vb_ref[:, 2 * q, :] = z_even
            vb_ref[:, 2 * q + 1, :] = z_odd
        tmp_ref[...] = transposed_pass(x_ref)
        ix_out[it] = permute(tmp_ref[ODD, :], mx_ref[...], True)
        ix = send(ix_out.at[it], ix_in.at[it], 4 * it + 2, x_next)
        turned = transposed_pass(y_ref)
        iy_out[it] = swap_pairs(turned.T[120:128], yswap)
        iy = send(iy_out.at[it], iy_in.at[it], 4 * it + 3, y_next)
        acc_ref[...] = diag_ref[...] * z + jnp.where(lane == 0, 0.0, pltpu.roll(turned, 1, 1))
        acc_ref[ODD, :] += tmp_ref[EVEN, :]
        between()
        acc_ref[...] += both_pass(e_ref, z, True)
        flat = permute(jnp.concatenate([z_even, z_odd], axis=1), mp_ref[...], False)
        tmp_ref[EVEN, :] = flat[:, :128]
        tmp_ref[ODD, :] = flat[:, 128:]
        tmp_ref[...] = both_pass(p_ref, tmp_ref[...], False)
        flat = permute(jnp.concatenate([tmp_ref[EVEN, :], tmp_ref[ODD, :]], axis=1), mp_ref[...], True)
        acc_ref[EVEN, :] += flat[:, :128]
        acc_ref[ODD, :] += flat[:, 128:]
        hx.wait_recv()
        tmp_ref[EVEN, :] = z_odd
        tmp_ref[ODD, :] = permute(hx_in[it], mx_ref[...], False) * edge_x
        forward_pass(x_ref, tmp_ref[...])
        hy.wait_recv()
        beyond = column(swap_pairs(hy_in[it], yswap)[0:1]) * edge_y
        forward_pass(y_ref, jnp.where(lane == 127, beyond, pltpu.roll(z, 127, 1)))
        for a, part in ((0, EVEN), (1, ODD)):
            total = red_ref[:, a, :]
            for q in range(1, 4):
                total = total + red_ref[:, 2 * q + a, :]
            acc_ref[part, :] += total
        ix.wait_recv()
        acc_ref[EVEN, :] += ix_in[it] * start_x
        iy.wait_recv()
        acc_ref[...] += jnp.where(lane == 0, column(iy_in[it, 7:8]) * start_y, 0.0)
        sent.extend([hx, hy, ix, iy])
        return acc_ref[...]

    u_ref[...] = residual_ref[...] / jac_ref[...]
    w_ref[...] = apply(0, u_ref[...], lambda: None)
    alpha = gamma_old = None
    for it in range(ITERS):
        last = it + 1 == ITERS
        sum_begin(it, residual_ref[...] * u_ref[...], w_ref[...] * u_ref[...])
        if last:
            sum_middle(it)
        else:
            m = w_ref[...] / jac_ref[...]
            n = apply(it + 1, m, functools.partial(sum_middle, it))
        gamma, delta = sum_end(it)
        if it == 0:
            alpha = gamma / delta
            direction, image = u_ref[...], w_ref[...]
            adjoint_ref[...] = alpha * direction
        else:
            beta = gamma / gamma_old
            alpha = gamma / (delta - beta * gamma / alpha)
            direction = u_ref[...] + beta * d_ref[...]
            image = w_ref[...] + beta * s_ref[...]
            adjoint_ref[...] += alpha * direction
            if not last:
                m = m + beta * q_ref[...]
                n = n + beta * zz_ref[...]
        gamma_old = gamma
        residual_ref[...] -= alpha * image
        if not last:
            d_ref[...] = direction
            s_ref[...] = image
            q_ref[...] = m
            zz_ref[...] = n
            u_ref[...] -= alpha * m
            w_ref[...] -= alpha * n

    for copy in sent:
        copy.wait_send()
    for it in range(ITERS):
        for stage, (buffer, count) in enumerate([(sum_a, 7), (sum_b, 15)]):
            mover = buffer.at[it, pl.ds(0, count)]
            pltpu.make_async_copy(mover, mover, sum_send.at[it, stage]).wait()
    pltpu.make_async_copy(prod_ref.at[pl.ds(0, 28)], prod_ref.at[pl.ds(0, 28)], ring_send).wait()
    pltpu.make_async_copy(plane_ref.at[pl.ds(0, 15)], plane_ref.at[pl.ds(0, 15)], plane_sem.at[0]).wait()
    pltpu.make_async_copy(index_ref.at[pl.ds(0, 15)], index_ref.at[pl.ds(0, 15)], index_sem.at[0]).wait()


def local(*args):
    (
        quad_features,
        w_first,
        w_second,
        w_third,
        quad_block,
        diag_tiles,
        x_tiles,
        y_tiles,
        p_tiles,
        tile_cols,
        x_map,
        y_map,
    ) = args
    features = quad_features.reshape(16384, FEATURES)
    tiles = [t.reshape(64, 128, 128) for t in (diag_tiles, x_tiles, y_tiles, p_tiles)]
    owners = quad_block.reshape(128, 128)
    cols = jnp.broadcast_to(tile_cols.reshape(1, 256), (8, 256))
    xmap = jnp.broadcast_to(x_map.reshape(1, 128), (8, 128))
    yswap = jnp.broadcast_to(y_map[0, 0, 0], (8, 128))
    hbm = pl.BlockSpec(memory_space=pl.ANY)
    vmem = pl.BlockSpec(memory_space=pltpu.VMEM)
    square = pltpu.VMEM((128, 128), F32)
    tile = pltpu.VMEM((64, 128, 128), F32)
    halves = pltpu.VMEM((ITERS, 64, 128), F32)
    strip = pltpu.VMEM((ITERS, 8, 128), F32)
    dma = pltpu.SemaphoreType.DMA
    adjoint, residual = pl.pallas_call(
        kernel,
        out_shape=[jax.ShapeDtypeStruct((128, 128), F32)] * 2,
        in_specs=[hbm, vmem, vmem, vmem, vmem, hbm, hbm, hbm, hbm, vmem, vmem, vmem],
        out_specs=[vmem, vmem],
        scratch_shapes=[
            pltpu.VMEM((16384, FEATURES), BF16),
            pltpu.VMEM((64, 512), BF16),
            pltpu.VMEM((512, 512), BF16),
            pltpu.VMEM((32, 4, 128, 128), BF16),
            pltpu.VMEM((8, 16, 128, 128), BF16),
            pltpu.VMEM((16, 256, 128), BF16),
            pltpu.VMEM((16, 256, 128), BF16),
            pltpu.VMEM((16, 8, 128), jnp.int32),
            pltpu.VMEM((16, 8, 128), jnp.int32),
            tile,
            tile,
            tile,
            tile,
            pltpu.VMEM((256, 256), BF16),
            pltpu.VMEM((128, 128), BF16),
            pltpu.VMEM((8, 128, 128), F32),
            pltpu.VMEM((64, 8, 128), F32),
            pltpu.VMEM((64, 8, 128), F32),
            square,
            square,
            halves,
            strip,
            halves,
            strip,
            halves,
            strip,
            halves,
            strip,
            pltpu.VMEM((ITERS, 8, 2, 128), F32),
            pltpu.VMEM((ITERS, 16, 2, 128), F32),
            dma((5,)),
            dma,
            dma((8,)),
            dma((2,)),
            dma((2,)),
            dma((4 * ITERS,)),
            dma((4 * ITERS,)),
            dma((ITERS, 2)),
            dma((ITERS, 2)),
        ],
        compiler_params=pltpu.CompilerParams(
            collective_id=0, has_side_effects=True, vmem_limit_bytes=56 * 2**20
        ),
    )(features, w_first, w_second, w_third, owners, *tiles, cols, xmap, yswap)
    return adjoint.reshape(64, 2, 128), residual.reshape(64, 2, 128)


def solution(mesh):
    in_specs = (
        P("sx", "sy", None, None),
        P(),
        P(),
        P(),
        P("sx", "sy", None),
        P(None, None, "sx", "sy"),
        P(None, None, "sx", "sy"),
        P(None, None, "sx", "sy"),
        P(None, None, "sx", "sy"),
        P("sx", "sy", None),
        P("sx", "sy", None),
        P("sx", "sy", None),
    )
    out_specs = (P(None, "sx", "sy"), P(None, "sx", "sy"))
    return jax.shard_map(local, mesh=mesh, in_specs=in_specs, out_specs=out_specs, check_vma=False)
```

```python
import functools

import jax
import jax.numpy as jnp
from jax import lax
from jax.experimental import pallas as pl
from jax.experimental.pallas import tpu as pltpu
from jax.sharding import PartitionSpec as P

FEATURES = 64
ITERS = 3
PER_BLOCK = 64
DIAG_SHIFT = 5.0
MESH = pl.DeviceIdType.MESH
F32 = jnp.float32
BF16 = jnp.bfloat16
EVEN = pl.ds(0, 64, stride=2)
ODD = pl.ds(1, 64, stride=2)


def permute(value, matrix, transposed):
    rows = value.shape[0]
    high = value.astype(BF16)
    rest = value - high.astype(F32)
    middle = rest.astype(BF16)
    low = (rest - middle.astype(F32)).astype(BF16)
    parts = jnp.concatenate([high, middle, low], axis=0)
    dims = (((1,), (1 if transposed else 0,)), ((), ()))
    product = lax.dot_general(parts, matrix, dims, preferred_element_type=F32)
    return product[:rows] + product[rows : 2 * rows] + product[2 * rows :]


def swap_pairs(row, swap):
    lane = lax.broadcasted_iota(jnp.int32, row.shape, 1)
    swapped = jnp.where(lane % 2 == 0, pltpu.roll(row, 127, 1), pltpu.roll(row, 1, 1))
    return jnp.where(swap > 0, swapped, row)


def column(row):
    return jnp.broadcast_to(row, (128, 128)).T


def silu_of_half(u):
    return (u + u * jnp.tanh(u)).astype(BF16)


def kernel(
    feat_hbm,
    w1_ref,
    w2_ref,
    w3_ref,
    owner_ref,
    diag_hbm,
    x_hbm,
    y_hbm,
    p_hbm,
    cols_ref,
    xmap_ref,
    yswap_ref,
    adjoint_ref,
    residual_ref,
    feat_ref,
    w1t_ref,
    w2t_ref,
    w3t_ref,
    prod_ref,
    ring_ref,
    plane_out,
    plane_ref,
    index_out,
    index_ref,
    e_ref,
    x_ref,
    y_ref,
    p_ref,
    mp_ref,
    mx_ref,
    vectors,
    vb_ref,
    red_ref,
    acc_ref,
    tmp_ref,
    hx_out,
    hy_out,
    ix_out,
    iy_out,
    hx_in,
    hy_in,
    ix_in,
    iy_in,
    sum_a,
    sum_b,
    local_sem,
    ring_send,
    ring_recv,
    plane_sem,
    index_sem,
    halo_send,
    halo_recv,
    sum_send,
    sum_recv,
):
    i = lax.axis_index("sx")
    j = lax.axis_index("sy")
    y, zh = i // 2, lax.rem(i, 2)
    zl, jl = j // 8, lax.rem(j, 8)
    x, core = jl // 2, lax.rem(j, 2)

    loads = [
        pltpu.make_async_copy(src, dst, local_sem.at[k])
        for k, (src, dst) in enumerate(
            [(feat_hbm, feat_ref), (diag_hbm, e_ref), (x_hbm, x_ref), (y_hbm, y_ref), (p_hbm, p_ref)]
        )
    ]
    for load in loads:
        load.start()

    def pick(first, second):
        return first * (1 - core) + second * core

    others = [(i, lax.rem(j + k, 16)) for k in range(1, 16)]
    others += [(lax.rem(i + k, 8), j) for k in range(1, 8)]
    others += [(lax.rem(i + k, 8), lax.rem(j + 8, 16)) for k in range(1, 8)]
    others += [(lax.rem(y + k, 4) * 2 + zh, j + 1 - 2 * core) for k in range(1, 4)]
    others += [(y * 2 + 1 - zh, lax.rem(j + 2 * k, 16)) for k in range(1, 8)]
    barrier = pltpu.get_barrier_semaphore()
    for other in others:
        pl.semaphore_signal(barrier, inc=1, device_id=other, device_id_type=MESH)

    w1t_ref[...] = (w1_ref[...].astype(F32) * 0.5).T.astype(BF16)
    w2t_ref[...] = (w2_ref[...].astype(F32) * 0.5).T.astype(BF16)
    w3t_ref[...] = w3_ref[...].astype(F32).T.astype(BF16)

    place_yz, place_xz = i * 2 + zl, zh * 8 + zl * 4 + x
    place = pick(place_yz, place_xz)

    def plane_device(t):
        return pick(t // 2, y * 2 + t // 8), pick(lax.rem(t, 2) * 8 + x * 2, lax.rem(t, 8) * 2 + 1)

    for t in range(16):
        for q in range(4):
            first = pick((t // 2) * 16 + (t % 2) * 8 + q * 2, (q * 2 + t // 8) * 16 + (t % 8) * 2)
            index_out[t, 2 * q : 2 * q + 2, :] = owner_ref[pl.ds(first, 2), :]
    index_ref[place] = index_out[place]

    def send_index(s, carry):
        t = lax.rem(place + s, 16)
        pltpu.make_async_remote_copy(
            src_ref=index_out.at[t],
            dst_ref=index_ref.at[place],
            send_sem=index_sem.at[0],
            recv_sem=index_sem.at[1],
            device_id=plane_device(t),
            device_id_type=MESH,
        ).start()
        return carry

    mp_ref[...] = (lax.broadcasted_iota(jnp.int32, (256, 256), 0) == cols_ref[0:1]).astype(F32).astype(BF16)
    mx_ref[...] = (lax.broadcasted_iota(jnp.int32, (128, 128), 0) == xmap_ref[0:1]).astype(F32).astype(BF16)
    yswap = yswap_ref[0:1, 0:1]

    loads[0].wait()

    def chunk(c, part):
        for half in range(2):
            columns = []
            for q in (2 * half, 2 * half + 1):
                _, dcore, dx, dy = ring_device(c, q)
                for u in range(4):
                    t = lax.rem((1 - dcore) * place_yz + dcore * place_xz + part * 4 + u, 16)
                    ri = (1 - dcore) * (t // 2) + dcore * (dy * 2 + t // 8)
                    rj = (1 - dcore) * (lax.rem(t, 2) * 8 + dx * 2) + dcore * (lax.rem(t, 8) * 2 + 1)
                    start = pl.multiple_of((ri * 16 + rj) * 128, 128)
                    columns.append(feat_ref[:, pl.ds(start, 128)])
            columns = jnp.concatenate(columns, axis=1)
            hidden = silu_of_half(jnp.dot(w1t_ref[...], columns, preferred_element_type=F32))
            hidden = silu_of_half(jnp.dot(w2t_ref[...], hidden, preferred_element_type=F32))
            output = jnp.dot(w3t_ref[...], hidden, preferred_element_type=F32)
            stress, tangent = output[:64], output[64:]
            tangent = jnp.maximum(tangent, 0.0) + jnp.log(1.0 + jnp.exp(-jnp.abs(tangent)))
            output = jnp.concatenate([stress, tangent * (1.0 / PER_BLOCK)], axis=0).astype(BF16)
            for u in range(8):
                prod_ref[part * 2 + c, 2 * half + u // 4, u % 4] = output[:, u * 128 : (u + 1) * 128]

        @pl.when(part * 2 + c == 0)
        def _():
            pl.semaphore_wait(barrier, len(others))
            lax.fori_loop(1, 16, send_index, 0)

        for q in range(4):
            turn, dcore, dx, dy = ring_device(c, q)
            slot = (1 - dcore) * (x * 2 + core) + dcore * (y * 2 + core)

            def remote():
                pltpu.make_async_remote_copy(
                    src_ref=prod_ref.at[part * 2 + c, q],
                    dst_ref=ring_ref.at[slot, part],
                    send_sem=ring_send,
                    recv_sem=ring_recv.at[slot, part],
                    device_id=(dy * 2 + zh, (zl * 4 + dx) * 2 + dcore),
                    device_id_type=MESH,
                ).start()

            if q < 3:
                remote()
            else:
                pl.when(c == 0)(remote)

                @pl.when(c == 1)
                def _():
                    ring_ref[slot, part] = prod_ref[part * 2 + c, q]

        return part

    def ring_device(c, q):
        turn = jnp.where(c == 0, (1, 1, 3, 3)[q], (2, 2, 0, 0)[q])
        dcore = lax.rem(core + jnp.where(c == 0, (0, 1, 0, 1)[q], (0, 1, 1, 0)[q]), 2)
        return turn, dcore, lax.rem(x + turn * (1 - dcore), 4), lax.rem(y + turn * dcore, 4)

    mine = pick(x * 2 + core, y * 2 + core)

    def reduce_rows(part):
        @pl.when(part == 0)
        def _():
            got = index_ref.at[pl.ds(0, 15)]
            pltpu.make_async_copy(got, got, index_sem.at[1]).wait()

        for s in range(1, 8):
            slot = lax.rem(mine + s, 8)
            got = ring_ref.at[slot, part]
            pltpu.make_async_copy(got, got, ring_recv.at[slot, part]).wait()

        def one(u, carry):
            t = lax.rem(place + part * 4 + u, 16)
            owners = index_ref[t]
            block = lax.broadcasted_iota(jnp.int32, (256, 128), 0)
            onehot = jnp.concatenate(
                [(block == owners[e : e + 1]).astype(F32).astype(BF16) for e in range(8)], axis=1
            )
            rows = jnp.concatenate([ring_ref[e, part, u] for e in range(8)], axis=1)
            plane_out[t] = lax.dot_general(
                rows, onehot, (((1,), (1,)), ((), ())), preferred_element_type=F32
            ).astype(BF16)

            @pl.when(part * 4 + u > 0)
            def _():
                pltpu.make_async_remote_copy(
                    src_ref=plane_out.at[t],
                    dst_ref=plane_ref.at[place],
                    send_sem=plane_sem.at[0],
                    recv_sem=plane_sem.at[1],
                    device_id=plane_device(t),
                    device_id_type=MESH,
                ).start()

            @pl.when(part * 4 + u == 0)
            def _():
                plane_ref[place] = plane_out[t]

            return carry

        lax.fori_loop(0, 4, one, 0)

    def run_part(part, carry):
        lax.fori_loop(0, 2, chunk, part)

        @pl.when(part > 0)
        def _():
            reduce_rows(part - 1)

        return carry

    lax.fori_loop(0, 4, run_part, 0)
    reduce_rows(jnp.int32(3))
    for load in loads[1:]:
        load.wait()
    jac_ref, diag_ref, u_ref, w_ref, d_ref, s_ref, q_ref, zz_ref = (vectors.at[k] for k in range(8))
    for k in range(64):
        jac_ref[2 * k : 2 * k + 2, :] = e_ref[k, 2 * k : 2 * k + 2, :]
    pltpu.make_async_copy(plane_ref.at[pl.ds(0, 15)], plane_ref.at[pl.ds(0, 15)], plane_sem.at[1]).wait()
    total = plane_ref[0].astype(F32)
    for t in range(1, 16):
        total = total + plane_ref[t].astype(F32)
    fields = total
    residual_ref[EVEN, :] = fields[:64, :128]
    residual_ref[ODD, :] = fields[:64, 128:]
    diag_ref[EVEN, :] = fields[64:, :128] + DIAG_SHIFT
    diag_ref[ODD, :] = fields[64:, 128:] + DIAG_SHIFT
    jac_ref[...] = diag_ref[...] + 2.0 * jac_ref[...]

    x_next, x_prev = (lax.rem(i + 1, 8), j), (lax.rem(i + 7, 8), j)
    y_next, y_prev = (i, lax.rem(j + 1, 16)), (i, lax.rem(j + 15, 16))
    lane = lax.broadcasted_iota(jnp.int32, (128, 128), 1)
    edge_x = jnp.where(i == 7, 0.0, 1.0)
    edge_y = jnp.where(j == 15, 0.0, 1.0)
    start_x = jnp.where(i == 0, 0.0, 1.0)
    start_y = jnp.where(j == 0, 0.0, 1.0)

    def send(src, dst, slot, to):
        copy = pltpu.make_async_remote_copy(
            src_ref=src,
            dst_ref=dst,
            send_sem=halo_send.at[slot],
            recv_sem=halo_recv.at[slot],
            device_id=to,
            device_id_type=MESH,
        )
        copy.start()
        return copy

    def transposed_pass(tiles):
        def body(step, total):
            for u in range(2):
                k = step * 2 + u
                total = total + tiles[k].reshape(16, 8, 128) * vb_ref[k][None]
            return total

        return lax.fori_loop(0, 32, body, jnp.zeros((16, 8, 128), F32)).reshape(128, 128)

    def forward_pass(tiles, partner):
        partner = partner.reshape(16, 8, 128)

        def body(step, carry):
            for u in range(2):
                k = step * 2 + u
                red_ref[k] += jnp.sum(tiles[k].reshape(16, 8, 128) * partner, axis=0)
            return carry

        lax.fori_loop(0, 32, body, 0)

    def both_pass(tiles, partner, first):
        partner = partner.reshape(16, 8, 128)

        def body(step, total):
            for u in range(2):
                k = step * 2 + u
                tile = tiles[k].reshape(16, 8, 128)
                forward = jnp.sum(tile * partner, axis=0)
                red_ref[k] = forward if first else red_ref[k] + forward
                total = total + tile * vb_ref[k][None]
            return total

        return lax.fori_loop(0, 32, body, jnp.zeros((16, 8, 128), F32)).reshape(128, 128)

    index_b = i * 2 + zl

    def sum_begin(it, first, second):
        sum_a[it, jl] = jnp.concatenate(
            [jnp.sum(first, axis=0, keepdims=True), jnp.sum(second, axis=0, keepdims=True)], axis=0
        )
        for k in range(1, 8):
            pltpu.make_async_remote_copy(
                src_ref=sum_a.at[it, jl],
                dst_ref=sum_a.at[it, jl],
                send_sem=sum_send.at[it, 0],
                recv_sem=sum_recv.at[it, 0],
                device_id=(i, zl * 8 + lax.rem(jl + k, 8)),
                device_id_type=MESH,
            ).start()

    def sum_middle(it):
        pltpu.make_async_copy(sum_a.at[it, pl.ds(0, 7)], sum_a.at[it, pl.ds(0, 7)], sum_recv.at[it, 0]).wait()
        sum_b[it, index_b] = jnp.sum(sum_a[it], axis=0)
        for k in range(1, 16):
            peer = lax.rem(index_b + k, 16)
            pltpu.make_async_remote_copy(
                src_ref=sum_b.at[it, index_b],
                dst_ref=sum_b.at[it, index_b],
                send_sem=sum_send.at[it, 1],
                recv_sem=sum_recv.at[it, 1],
                device_id=(peer // 2, lax.rem(peer, 2) * 8 + jl),
                device_id_type=MESH,
            ).start()

    def sum_end(it):
        pltpu.make_async_copy(sum_b.at[it, pl.ds(0, 15)], sum_b.at[it, pl.ds(0, 15)], sum_recv.at[it, 1]).wait()
        total = jnp.sum(jnp.sum(sum_b[it], axis=0), axis=1, keepdims=True)
        return total[0:1], total[1:2]

    sent = []

    def apply(it, z, between):
        tmp_ref[...] = z
        z_even, z_odd = tmp_ref[EVEN, :], tmp_ref[ODD, :]
        hx_out[it] = z_even
        hx = send(hx_out.at[it], hx_in.at[it], 4 * it, x_prev)
        hy_out[it] = z.T[0:8]
        hy = send(hy_out.at[it], hy_in.at[it], 4 * it + 1, y_prev)
        for q in range(4):
            vb_ref[:, 2 * q, :] = z_even
            vb_ref[:, 2 * q + 1, :] = z_odd
        tmp_ref[...] = transposed_pass(x_ref)
        ix_out[it] = permute(tmp_ref[ODD, :], mx_ref[...], True)
        ix = send(ix_out.at[it], ix_in.at[it], 4 * it + 2, x_next)
        turned = transposed_pass(y_ref)
        iy_out[it] = swap_pairs(turned.T[120:128], yswap)
        iy = send(iy_out.at[it], iy_in.at[it], 4 * it + 3, y_next)
        acc_ref[...] = diag_ref[...] * z + jnp.where(lane == 0, 0.0, pltpu.roll(turned, 1, 1))
        acc_ref[ODD, :] += tmp_ref[EVEN, :]
        between()
        acc_ref[...] += both_pass(e_ref, z, True)
        flat = permute(jnp.concatenate([z_even, z_odd], axis=1), mp_ref[...], False)
        tmp_ref[EVEN, :] = flat[:, :128]
        tmp_ref[ODD, :] = flat[:, 128:]
        tmp_ref[...] = both_pass(p_ref, tmp_ref[...], False)
        flat = permute(jnp.concatenate([tmp_ref[EVEN, :], tmp_ref[ODD, :]], axis=1), mp_ref[...], True)
        acc_ref[EVEN, :] += flat[:, :128]
        acc_ref[ODD, :] += flat[:, 128:]
        hx.wait_recv()
        tmp_ref[EVEN, :] = z_odd
        tmp_ref[ODD, :] = permute(hx_in[it], mx_ref[...], False) * edge_x
        forward_pass(x_ref, tmp_ref[...])
        hy.wait_recv()
        beyond = column(swap_pairs(hy_in[it], yswap)[0:1]) * edge_y
        forward_pass(y_ref, jnp.where(lane == 127, beyond, pltpu.roll(z, 127, 1)))
        for a, part in ((0, EVEN), (1, ODD)):
            total = red_ref[:, a, :]
            for q in range(1, 4):
                total = total + red_ref[:, 2 * q + a, :]
            acc_ref[part, :] += total
        ix.wait_recv()
        acc_ref[EVEN, :] += ix_in[it] * start_x
        iy.wait_recv()
        acc_ref[...] += jnp.where(lane == 0, column(iy_in[it, 7:8]) * start_y, 0.0)
        sent.extend([hx, hy, ix, iy])
        return acc_ref[...]

    u_ref[...] = residual_ref[...] / jac_ref[...]
    w_ref[...] = apply(0, u_ref[...], lambda: None)
    alpha = gamma_old = None
    for it in range(ITERS):
        last = it + 1 == ITERS
        sum_begin(it, residual_ref[...] * u_ref[...], w_ref[...] * u_ref[...])
        if last:
            sum_middle(it)
        else:
            m = w_ref[...] / jac_ref[...]
            n = apply(it + 1, m, functools.partial(sum_middle, it))
        gamma, delta = sum_end(it)
        if it == 0:
            alpha = gamma / delta
            direction, image = u_ref[...], w_ref[...]
            adjoint_ref[...] = alpha * direction
        else:
            beta = gamma / gamma_old
            alpha = gamma / (delta - beta * gamma / alpha)
            direction = u_ref[...] + beta * d_ref[...]
            image = w_ref[...] + beta * s_ref[...]
            adjoint_ref[...] += alpha * direction
            if not last:
                m = m + beta * q_ref[...]
                n = n + beta * zz_ref[...]
        gamma_old = gamma
        residual_ref[...] -= alpha * image
        if not last:
            d_ref[...] = direction
            s_ref[...] = image
            q_ref[...] = m
            zz_ref[...] = n
            u_ref[...] -= alpha * m
            w_ref[...] -= alpha * n

    for copy in sent:
        copy.wait_send()
    for it in range(ITERS):
        for stage, (buffer, count) in enumerate([(sum_a, 7), (sum_b, 15)]):
            mover = buffer.at[it, pl.ds(0, count)]
            pltpu.make_async_copy(mover, mover, sum_send.at[it, stage]).wait()
    out = prod_ref.at[pl.ds(0, 7)]
    pltpu.make_async_copy(out, out, ring_send).wait()
    pltpu.make_async_copy(plane_ref.at[pl.ds(0, 15)], plane_ref.at[pl.ds(0, 15)], plane_sem.at[0]).wait()
    pltpu.make_async_copy(index_ref.at[pl.ds(0, 15)], index_ref.at[pl.ds(0, 15)], index_sem.at[0]).wait()


def hand_over(adjoint_ref, residual_ref, adjoint_out, residual_out):
    adjoint_out[...] = adjoint_ref[...]
    residual_out[...] = residual_ref[...]


def local(*args):
    (
        quad_features,
        w_first,
        w_second,
        w_third,
        quad_block,
        diag_tiles,
        x_tiles,
        y_tiles,
        p_tiles,
        tile_cols,
        x_map,
        y_map,
    ) = args
    features = quad_features.reshape(16384, FEATURES).T
    tiles = [t.reshape(64, 128, 128) for t in (diag_tiles, x_tiles, y_tiles, p_tiles)]
    owners = quad_block.reshape(128, 128)
    cols = tile_cols.reshape(1, 256)
    xmap = x_map.reshape(1, 128)
    yswap = y_map.reshape(1, 2)
    hbm = pl.BlockSpec(memory_space=pl.ANY)
    vmem = pl.BlockSpec(memory_space=pltpu.VMEM)
    square = pltpu.VMEM((128, 128), F32)
    tile = pltpu.VMEM((64, 128, 128), F32)
    halves = pltpu.VMEM((ITERS, 64, 128), F32)
    strip = pltpu.VMEM((ITERS, 8, 128), F32)
    dma = pltpu.SemaphoreType.DMA
    adjoint, residual = pl.pallas_call(
        kernel,
        out_shape=[jax.ShapeDtypeStruct((128, 128), F32)] * 2,
        in_specs=[hbm, vmem, vmem, vmem, vmem, hbm, hbm, hbm, hbm, vmem, vmem, vmem],
        out_specs=[vmem, vmem],
        scratch_shapes=[
            pltpu.VMEM((FEATURES, 16384), BF16),
            pltpu.VMEM((512, 64), BF16),
            pltpu.VMEM((512, 512), BF16),
            pltpu.VMEM((128, 512), BF16),
            pltpu.VMEM((8, 4, 4, 128, 128), BF16),
            pltpu.VMEM((8, 4, 4, 128, 128), BF16),
            pltpu.VMEM((16, 128, 256), BF16),
            pltpu.VMEM((16, 128, 256), BF16),
            pltpu.VMEM((16, 8, 128), jnp.int32),
            pltpu.VMEM((16, 8, 128), jnp.int32),
            tile,
            tile,
            tile,
            tile,
            pltpu.VMEM((256, 256), BF16),
            pltpu.VMEM((128, 128), BF16),
            pltpu.VMEM((8, 128, 128), F32),
            pltpu.VMEM((64, 8, 128), F32),
            pltpu.VMEM((64, 8, 128), F32),
            square,
            square,
            halves,
            strip,
            halves,
            strip,
            halves,
            strip,
            halves,
            strip,
            pltpu.VMEM((ITERS, 8, 2, 128), F32),
            pltpu.VMEM((ITERS, 16, 2, 128), F32),
            dma((5,)),
            dma,
            dma((8, 4)),
            dma((2,)),
            dma((2,)),
            dma((4 * ITERS,)),
            dma((4 * ITERS,)),
            dma((ITERS, 2)),
            dma((ITERS, 2)),
        ],
        compiler_params=pltpu.CompilerParams(
            collective_id=0, has_side_effects=True, vmem_limit_bytes=56 * 2**20
        ),
    )(features, w_first, w_second, w_third, owners, *tiles, cols, xmap, yswap)
    adjoint, residual = pl.pallas_call(
        hand_over,
        out_shape=[jax.ShapeDtypeStruct((128, 128), F32)] * 2,
        in_specs=[vmem, vmem],
        out_specs=[vmem, vmem],
    )(adjoint, residual)
    return adjoint.reshape(64, 2, 128), residual.reshape(64, 2, 128)


def solution(mesh):
    in_specs = (
        P("sx", "sy", None, None),
        P(),
        P(),
        P(),
        P("sx", "sy", None),
        P(None, None, "sx", "sy"),
        P(None, None, "sx", "sy"),
        P(None, None, "sx", "sy"),
        P(None, None, "sx", "sy"),
        P("sx", "sy", None),
        P("sx", "sy", None),
        P("sx", "sy", None),
    )
    out_specs = (P(None, "sx", "sy"), P(None, "sx", "sy"))
    return jax.shard_map(local, mesh=mesh, in_specs=in_specs, out_specs=out_specs, check_vma=False)
```

```python
import functools

import jax
import jax.numpy as jnp
from jax import lax
from jax.experimental import pallas as pl
from jax.experimental.pallas import tpu as pltpu
from jax.sharding import PartitionSpec as P

FEATURES = 64
ITERS = 3
PER_BLOCK = 64
DIAG_SHIFT = 5.0
MESH = pl.DeviceIdType.MESH
F32 = jnp.float32
BF16 = jnp.bfloat16
EVEN = pl.ds(0, 64, stride=2)
ODD = pl.ds(1, 64, stride=2)


def permute(value, matrix, transposed):
    rows = value.shape[0]
    high = value.astype(BF16)
    rest = value - high.astype(F32)
    middle = rest.astype(BF16)
    low = (rest - middle.astype(F32)).astype(BF16)
    parts = jnp.concatenate([high, middle, low], axis=0)
    dims = (((1,), (1 if transposed else 0,)), ((), ()))
    product = lax.dot_general(parts, matrix, dims, preferred_element_type=F32)
    return product[:rows] + product[rows : 2 * rows] + product[2 * rows :]


def swap_pairs(row, swap):
    lane = lax.broadcasted_iota(jnp.int32, row.shape, 1)
    swapped = jnp.where(lane % 2 == 0, pltpu.roll(row, 127, 1), pltpu.roll(row, 1, 1))
    return jnp.where(swap > 0, swapped, row)


def column(row):
    return jnp.broadcast_to(row, (128, 128)).T


def silu_of_half(u):
    return (u + u * jnp.tanh(u)).astype(BF16)


def kernel(
    feat_hbm,
    w1_ref,
    w2_ref,
    w3_ref,
    owner_ref,
    diag_hbm,
    x_hbm,
    y_hbm,
    p_hbm,
    cols_ref,
    xmap_ref,
    yswap_ref,
    adjoint_ref,
    residual_ref,
    feat_ref,
    w1t_ref,
    w2t_ref,
    w3t_ref,
    prod_ref,
    ring_ref,
    plane_out,
    plane_ref,
    index_out,
    index_ref,
    e_ref,
    x_ref,
    y_ref,
    p_ref,
    mp_ref,
    mx_ref,
    vectors,
    vb_ref,
    red_ref,
    acc_ref,
    tmp_ref,
    hx_out,
    hy_out,
    ix_out,
    iy_out,
    hx_in,
    hy_in,
    ix_in,
    iy_in,
    sum_a,
    sum_b,
    local_sem,
    ring_send,
    ring_recv,
    plane_sem,
    index_sem,
    halo_send,
    halo_recv,
    sum_send,
    sum_recv,
):
    i = lax.axis_index("sx")
    j = lax.axis_index("sy")
    y, zh = i // 2, lax.rem(i, 2)
    zl, jl = j // 8, lax.rem(j, 8)
    x, core = jl // 2, lax.rem(j, 2)

    loads = [
        pltpu.make_async_copy(src, dst, local_sem.at[k])
        for k, (src, dst) in enumerate(
            [(feat_hbm, feat_ref), (diag_hbm, e_ref), (x_hbm, x_ref), (y_hbm, y_ref), (p_hbm, p_ref)]
        )
    ]
    for load in loads:
        load.start()

    def pick(first, second):
        return first * (1 - core) + second * core

    others = [(i, lax.rem(j + k, 16)) for k in range(1, 16)]
    others += [(lax.rem(i + k, 8), j) for k in range(1, 8)]
    others += [(lax.rem(i + k, 8), lax.rem(j + 8, 16)) for k in range(1, 8)]
    others += [(lax.rem(y + k, 4) * 2 + zh, j + 1 - 2 * core) for k in range(1, 4)]
    others += [(y * 2 + 1 - zh, lax.rem(j + 2 * k, 16)) for k in range(1, 8)]
    barrier = pltpu.get_barrier_semaphore()
    for other in others:
        pl.semaphore_signal(barrier, inc=1, device_id=other, device_id_type=MESH)

    w1t_ref[...] = (w1_ref[...].astype(F32) * 0.5).T.astype(BF16)
    w2t_ref[...] = (w2_ref[...].astype(F32) * 0.5).T.astype(BF16)
    w3t_ref[...] = w3_ref[...].astype(F32).T.astype(BF16)

    place_yz, place_xz = i * 2 + zl, zh * 8 + zl * 4 + x
    place = pick(place_yz, place_xz)

    def plane_device(t):
        return pick(t // 2, y * 2 + t // 8), pick(lax.rem(t, 2) * 8 + x * 2, lax.rem(t, 8) * 2 + 1)

    for t in range(16):
        for q in range(4):
            first = pick((t // 2) * 16 + (t % 2) * 8 + q * 2, (q * 2 + t // 8) * 16 + (t % 8) * 2)
            index_out[t, 2 * q : 2 * q + 2, :] = owner_ref[pl.ds(first, 2), :]
    index_ref[place] = index_out[place]

    def send_index(s, carry):
        t = lax.rem(place + s, 16)
        pltpu.make_async_remote_copy(
            src_ref=index_out.at[t],
            dst_ref=index_ref.at[place],
            send_sem=index_sem.at[0],
            recv_sem=index_sem.at[1],
            device_id=plane_device(t),
            device_id_type=MESH,
        ).start()
        return carry

    mp_ref[...] = (lax.broadcasted_iota(jnp.int32, (256, 256), 0) == cols_ref[0:1]).astype(F32).astype(BF16)
    mx_ref[...] = (lax.broadcasted_iota(jnp.int32, (128, 128), 0) == xmap_ref[0:1]).astype(F32).astype(BF16)
    yswap = yswap_ref[0:1, 0:1]

    loads[0].wait()

    def ring_device(q):
        turn = (1, 1, 3, 3, 2, 2, 0, 0)[q]
        dcore = (core, 1 - core, core, 1 - core, core, 1 - core, 1 - core, core)[q]
        return dcore, lax.rem(x + turn * (1 - dcore), 4), lax.rem(y + turn * dcore, 4)

    def network(part):
        for half in range(2):
            columns = []
            for q in range(4 * half, 4 * half + 4):
                dcore, dx, dy = ring_device(q)
                for u in range(2):
                    t = lax.rem((1 - dcore) * place_yz + dcore * place_xz + part * 2 + u, 16)
                    ri = (1 - dcore) * (t // 2) + dcore * (dy * 2 + t // 8)
                    rj = (1 - dcore) * (lax.rem(t, 2) * 8 + dx * 2) + dcore * (lax.rem(t, 8) * 2 + 1)
                    start = pl.multiple_of((ri * 16 + rj) * 128, 128)
                    columns.append(feat_ref[:, pl.ds(start, 128)])
            columns = jnp.concatenate(columns, axis=1)
            hidden = silu_of_half(jnp.dot(w1t_ref[...], columns, preferred_element_type=F32))
            hidden = silu_of_half(jnp.dot(w2t_ref[...], hidden, preferred_element_type=F32))
            output = jnp.dot(w3t_ref[...], hidden, preferred_element_type=F32)
            stress, tangent = output[:64], output[64:]
            tangent = jnp.maximum(tangent, 0.0) + jnp.log(1.0 + jnp.exp(-jnp.abs(tangent)))
            output = jnp.concatenate([stress, tangent * (1.0 / PER_BLOCK)], axis=0).astype(BF16)
            for u in range(8):
                prod_ref[part, 4 * half + u // 2, u % 2] = output[:, u * 128 : (u + 1) * 128]

        @pl.when(part == 0)
        def _():
            pl.semaphore_wait(barrier, len(others))
            lax.fori_loop(1, 16, send_index, 0)

        for q in range(8):
            dcore, dx, dy = ring_device(q)
            slot = (1 - dcore) * (x * 2 + core) + dcore * (y * 2 + core)
            if q == 7:
                ring_ref[slot, part] = prod_ref[part, q]
            else:
                pltpu.make_async_remote_copy(
                    src_ref=prod_ref.at[part, q],
                    dst_ref=ring_ref.at[slot, part],
                    send_sem=ring_send,
                    recv_sem=ring_recv.at[slot, part],
                    device_id=(dy * 2 + zh, (zl * 4 + dx) * 2 + dcore),
                    device_id_type=MESH,
                ).start()

    mine = pick(x * 2 + core, y * 2 + core)

    def reduce_rows(part):
        @pl.when(part == 0)
        def _():
            got = index_ref.at[pl.ds(0, 15)]
            pltpu.make_async_copy(got, got, index_sem.at[1]).wait()

        for s in range(1, 8):
            slot = lax.rem(mine + s, 8)
            got = ring_ref.at[slot, part]
            pltpu.make_async_copy(got, got, ring_recv.at[slot, part]).wait()
        for u in range(2):
            t = lax.rem(place + part * 2 + u, 16)
            owners = index_ref[t]
            block = lax.broadcasted_iota(jnp.int32, (256, 128), 0)
            onehot = jnp.concatenate(
                [(block == owners[e : e + 1]).astype(F32).astype(BF16) for e in range(8)], axis=1
            )
            rows = jnp.concatenate([ring_ref[e, part, u] for e in range(8)], axis=1)
            plane_out[t] = lax.dot_general(
                rows, onehot, (((1,), (1,)), ((), ())), preferred_element_type=F32
            ).astype(BF16)

        def remote(u):
            t = lax.rem(place + part * 2 + u, 16)
            pltpu.make_async_remote_copy(
                src_ref=plane_out.at[t],
                dst_ref=plane_ref.at[place],
                send_sem=plane_sem.at[0],
                recv_sem=plane_sem.at[1],
                device_id=plane_device(t),
                device_id_type=MESH,
            ).start()

        pl.when(part > 0)(functools.partial(remote, 0))
        remote(1)

        @pl.when(part == 0)
        def _():
            plane_ref[place] = plane_out[place]

    def run_part(part, carry):
        network(part)

        @pl.when(part > 1)
        def _():
            reduce_rows(part - 2)

        return carry

    lax.fori_loop(0, 8, run_part, 0)

    def run_rest(part, carry):
        reduce_rows(part)
        return carry

    lax.fori_loop(6, 8, run_rest, 0)
    for load in loads[1:]:
        load.wait()
    jac_ref, off_ref, sum_ref, *krylov = (vectors.at[k] for k in range(8))
    for k in range(64):
        jac_ref[2 * k : 2 * k + 2, :] = e_ref[k, 2 * k : 2 * k + 2, :]
    pltpu.make_async_copy(plane_ref.at[pl.ds(0, 15)], plane_ref.at[pl.ds(0, 15)], plane_sem.at[1]).wait()
    total = plane_ref[0].astype(F32)
    for t in range(1, 16):
        total = total + plane_ref[t].astype(F32)
    fields = total
    residual_ref[EVEN, :] = fields[:64, :128]
    residual_ref[ODD, :] = fields[:64, 128:]
    off_ref[...] = -2.0 * jac_ref[...]
    jac_ref[EVEN, :] = fields[64:, :128] + DIAG_SHIFT
    jac_ref[ODD, :] = fields[64:, 128:] + DIAG_SHIFT
    jac_ref[...] = jac_ref[...] - off_ref[...]

    x_next, x_prev = (lax.rem(i + 1, 8), j), (lax.rem(i + 7, 8), j)
    y_next, y_prev = (i, lax.rem(j + 1, 16)), (i, lax.rem(j + 15, 16))
    lane = lax.broadcasted_iota(jnp.int32, (128, 128), 1)
    edge_x = jnp.where(i == 7, 0.0, 1.0)
    edge_y = jnp.where(j == 15, 0.0, 1.0)
    start_x = jnp.where(i == 0, 0.0, 1.0)
    start_y = jnp.where(j == 0, 0.0, 1.0)

    def send(src, dst, slot, to):
        copy = pltpu.make_async_remote_copy(
            src_ref=src,
            dst_ref=dst,
            send_sem=halo_send.at[slot],
            recv_sem=halo_recv.at[slot],
            device_id=to,
            device_id_type=MESH,
        )
        copy.start()
        return copy

    def transposed_pass(tiles):
        def body(step, total):
            for u in range(2):
                k = step * 2 + u
                total = total + tiles[k].reshape(16, 8, 128) * vb_ref[k][None]
            return total

        return lax.fori_loop(0, 32, body, jnp.zeros((16, 8, 128), F32)).reshape(128, 128)

    def forward_pass(tiles, partner):
        partner = partner.reshape(16, 8, 128)

        def body(step, carry):
            for u in range(2):
                k = step * 2 + u
                red_ref[k] += jnp.sum(tiles[k].reshape(16, 8, 128) * partner, axis=0)
            return carry

        lax.fori_loop(0, 32, body, 0)

    def both_pass(tiles, partner, first):
        partner = partner.reshape(16, 8, 128)

        def body(step, total):
            for u in range(2):
                k = step * 2 + u
                tile = tiles[k].reshape(16, 8, 128)
                forward = jnp.sum(tile * partner, axis=0)
                red_ref[k] = forward if first else red_ref[k] + forward
                total = total + tile * vb_ref[k][None]
            return total

        return lax.fori_loop(0, 32, body, jnp.zeros((16, 8, 128), F32)).reshape(128, 128)

    index_b = i * 2 + zl

    def sum_begin(rows):
        sum_a[jl] = jnp.concatenate(
            [jnp.sum(row, axis=0, keepdims=True) for row in rows] + [jnp.zeros((8 - len(rows), 128), F32)], axis=0
        )
        for k in range(1, 8):
            pltpu.make_async_remote_copy(
                src_ref=sum_a.at[jl],
                dst_ref=sum_a.at[jl],
                send_sem=sum_send.at[0],
                recv_sem=sum_recv.at[0],
                device_id=(i, zl * 8 + lax.rem(jl + k, 8)),
                device_id_type=MESH,
            ).start()

    def sum_middle():
        pltpu.make_async_copy(sum_a.at[pl.ds(0, 7)], sum_a.at[pl.ds(0, 7)], sum_recv.at[0]).wait()
        sum_b[index_b] = jnp.sum(sum_a[...], axis=0)
        for k in range(1, 16):
            peer = lax.rem(index_b + k, 16)
            pltpu.make_async_remote_copy(
                src_ref=sum_b.at[index_b],
                dst_ref=sum_b.at[index_b],
                send_sem=sum_send.at[1],
                recv_sem=sum_recv.at[1],
                device_id=(peer // 2, lax.rem(peer, 2) * 8 + jl),
                device_id_type=MESH,
            ).start()

    def sum_end():
        pltpu.make_async_copy(sum_b.at[pl.ds(0, 15)], sum_b.at[pl.ds(0, 15)], sum_recv.at[1]).wait()
        total = jnp.sum(jnp.sum(sum_b[...], axis=0), axis=1, keepdims=True)
        return [total[k : k + 1] for k in range(2 * ITERS)]

    sent = []

    def gather_p(even, odd, transposed):
        flat = permute(jnp.concatenate([even, odd], axis=1), mp_ref[...], transposed)
        return flat[:, :128], flat[:, 128:]

    def out_x(it):
        tmp_ref[...] = transposed_pass(x_ref)
        ix_out[it] = permute(tmp_ref[ODD, :], mx_ref[...], True)
        sent.append(send(ix_out.at[it], ix_in.at[it], 4 * it + 2, x_next))
        acc_ref[ODD, :] += tmp_ref[EVEN, :]
        return sent[-1]

    def out_y(it):
        turned = transposed_pass(y_ref)
        iy_out[it] = swap_pairs(turned.T[120:128], yswap)
        sent.append(send(iy_out.at[it], iy_in.at[it], 4 * it + 3, y_next))
        acc_ref[...] += jnp.where(lane == 0, 0.0, pltpu.roll(turned, 1, 1))
        return sent[-1]

    def couple(it, z, moments):
        last = it + 1 == ITERS
        tmp_ref[...] = z
        z_even, z_odd = tmp_ref[EVEN, :], tmp_ref[ODD, :]
        hx_out[it] = z_even
        hx = send(hx_out.at[it], hx_in.at[it], 4 * it, x_prev)
        hy_out[it] = z.T[0:8]
        hy = send(hy_out.at[it], hy_in.at[it], 4 * it + 1, y_prev)
        for q in range(4):
            vb_ref[:, 2 * q, :] = z_even
            vb_ref[:, 2 * q + 1, :] = z_odd
        acc_ref[...] = off_ref[...] * z
        if not last:
            ix, iy = out_x(it), out_y(it)
        acc_ref[...] += both_pass(e_ref, z, True)
        tmp_ref[EVEN, :], tmp_ref[ODD, :] = gather_p(z_even, z_odd, False)
        tmp_ref[...] = both_pass(p_ref, tmp_ref[...], False)
        add_even, add_odd = gather_p(tmp_ref[EVEN, :], tmp_ref[ODD, :], True)
        acc_ref[EVEN, :] += add_even
        acc_ref[ODD, :] += add_odd
        hx.wait_recv()
        tmp_ref[EVEN, :] = z_odd
        tmp_ref[ODD, :] = permute(hx_in[it], mx_ref[...], False) * edge_x
        forward_pass(x_ref, tmp_ref[...])
        hy.wait_recv()
        beyond = column(swap_pairs(hy_in[it], yswap)[0:1]) * edge_y
        forward_pass(y_ref, jnp.where(lane == 127, beyond, pltpu.roll(z, 127, 1)))
        for a, part in ((0, EVEN), (1, ODD)):
            total = red_ref[:, a, :]
            for q in range(1, 4):
                total = total + red_ref[:, 2 * q + a, :]
            sum_ref[part, :] = total
        acc_ref[...] += sum_ref[...]
        if last:
            sum_begin(moments + [z * (off_ref[...] * z + 2.0 * sum_ref[...])])
            ix, iy = out_x(it), out_y(it)
            sum_middle()
        ix.wait_recv()
        acc_ref[EVEN, :] += ix_in[it] * start_x
        iy.wait_recv()
        acc_ref[...] += jnp.where(lane == 0, column(iy_in[it, 7:8]) * start_y, 0.0)
        sent.extend([hx, hy])
        return acc_ref[...]

    v_refs, r_refs = krylov[:ITERS], [residual_ref] + krylov[ITERS:]
    moments = []
    for it in range(ITERS):
        v_refs[it][...] = r_refs[it][...] / jac_ref[...]
        moments.append(r_refs[it][...] * v_refs[it][...])
        image = couple(it, v_refs[it][...], moments)
        if it + 1 < ITERS:
            r_refs[it + 1][...] = image
            moments.append(image * v_refs[it][...])
    nu = sum_end()

    def ratio(above, below):
        return jnp.where(below == 0.0, 0.0, above / jnp.where(below == 0.0, 1.0, below))

    def form(first, second):
        return sum(a * b * nu[k + m] for k, a in enumerate(first) for m, b in enumerate(second))

    one = jnp.ones((1, 1), F32)
    res, direction, solved = [one], [one], [0.0] * ITERS
    gamma = nu[0]
    for it in range(ITERS):
        moved = [a + b for a, b in zip(direction + [0.0 * one], [0.0 * one] + direction)]
        alpha = ratio(gamma, form(direction, moved))
        solved = [a + alpha * b for a, b in zip(solved, direction)] + solved[len(direction) :]
        res = [a - alpha * b for a, b in zip(res + [0.0 * one], moved)]
        if it + 1 < ITERS:
            gamma_next = form(res, res)
            beta = ratio(gamma_next, gamma)
            direction = [a + beta * b for a, b in zip(res, direction + [0.0 * one])]
            gamma = gamma_next
    adjoint_ref[...] = sum(a * v[...] for a, v in zip(solved, v_refs))
    residual_ref[...] = sum(a * r[...] for a, r in zip(res, r_refs)) + res[ITERS] * image

    for copy in sent:
        copy.wait_send()
    for stage, (buffer, count) in enumerate([(sum_a, 7), (sum_b, 15)]):
        mover = buffer.at[pl.ds(0, count)]
        pltpu.make_async_copy(mover, mover, sum_send.at[stage]).wait()
    out = prod_ref.at[pl.ds(0, 7)]
    pltpu.make_async_copy(out, out, ring_send).wait()
    pltpu.make_async_copy(plane_ref.at[pl.ds(0, 15)], plane_ref.at[pl.ds(0, 15)], plane_sem.at[0]).wait()
    pltpu.make_async_copy(index_ref.at[pl.ds(0, 15)], index_ref.at[pl.ds(0, 15)], index_sem.at[0]).wait()


def hand_over(adjoint_ref, residual_ref, adjoint_out, residual_out):
    adjoint_out[...] = adjoint_ref[...]
    residual_out[...] = residual_ref[...]


def local(*args):
    (
        quad_features,
        w_first,
        w_second,
        w_third,
        quad_block,
        diag_tiles,
        x_tiles,
        y_tiles,
        p_tiles,
        tile_cols,
        x_map,
        y_map,
    ) = args
    features = quad_features.reshape(16384, FEATURES).T
    tiles = [t.reshape(64, 128, 128) for t in (diag_tiles, x_tiles, y_tiles, p_tiles)]
    owners = quad_block.reshape(128, 128)
    cols = tile_cols.reshape(1, 256)
    xmap = x_map.reshape(1, 128)
    yswap = y_map.reshape(1, 2)
    hbm = pl.BlockSpec(memory_space=pl.ANY)
    vmem = pl.BlockSpec(memory_space=pltpu.VMEM)
    square = pltpu.VMEM((128, 128), F32)
    tile = pltpu.VMEM((64, 128, 128), F32)
    halves = pltpu.VMEM((ITERS, 64, 128), F32)
    strip = pltpu.VMEM((ITERS, 8, 128), F32)
    dma = pltpu.SemaphoreType.DMA
    adjoint, residual = pl.pallas_call(
        kernel,
        out_shape=[jax.ShapeDtypeStruct((128, 128), F32)] * 2,
        in_specs=[hbm, vmem, vmem, vmem, vmem, hbm, hbm, hbm, hbm, vmem, vmem, vmem],
        out_specs=[vmem, vmem],
        scratch_shapes=[
            pltpu.VMEM((FEATURES, 16384), BF16),
            pltpu.VMEM((512, 64), BF16),
            pltpu.VMEM((512, 512), BF16),
            pltpu.VMEM((128, 512), BF16),
            pltpu.VMEM((8, 8, 2, 128, 128), BF16),
            pltpu.VMEM((8, 8, 2, 128, 128), BF16),
            pltpu.VMEM((16, 128, 256), BF16),
            pltpu.VMEM((16, 128, 256), BF16),
            pltpu.VMEM((16, 8, 128), jnp.int32),
            pltpu.VMEM((16, 8, 128), jnp.int32),
            tile,
            tile,
            tile,
            tile,
            pltpu.VMEM((256, 256), BF16),
            pltpu.VMEM((128, 128), BF16),
            pltpu.VMEM((8, 128, 128), F32),
            pltpu.VMEM((64, 8, 128), F32),
            pltpu.VMEM((64, 8, 128), F32),
            square,
            square,
            halves,
            strip,
            halves,
            strip,
            halves,
            strip,
            halves,
            strip,
            pltpu.VMEM((8, 8, 128), F32),
            pltpu.VMEM((16, 8, 128), F32),
            dma((5,)),
            dma,
            dma((8, 8)),
            dma((2,)),
            dma((2,)),
            dma((4 * ITERS,)),
            dma((4 * ITERS,)),
            dma((2,)),
            dma((2,)),
        ],
        compiler_params=pltpu.CompilerParams(
            collective_id=0, has_side_effects=True, vmem_limit_bytes=56 * 2**20
        ),
    )(features, w_first, w_second, w_third, owners, *tiles, cols, xmap, yswap)
    adjoint, residual = pl.pallas_call(
        hand_over,
        out_shape=[jax.ShapeDtypeStruct((128, 128), F32)] * 2,
        in_specs=[vmem, vmem],
        out_specs=[vmem, vmem],
    )(adjoint, residual)
    return adjoint.reshape(64, 2, 128), residual.reshape(64, 2, 128)


def solution(mesh):
    in_specs = (
        P("sx", "sy", None, None),
        P(),
        P(),
        P(),
        P("sx", "sy", None),
        P(None, None, "sx", "sy"),
        P(None, None, "sx", "sy"),
        P(None, None, "sx", "sy"),
        P(None, None, "sx", "sy"),
        P("sx", "sy", None),
        P("sx", "sy", None),
        P("sx", "sy", None),
    )
    out_specs = (P(None, "sx", "sy"), P(None, "sx", "sy"))
    return jax.shard_map(local, mesh=mesh, in_specs=in_specs, out_specs=out_specs, check_vma=False)
```

```python
import functools

import jax
import jax.numpy as jnp
from jax import lax
from jax.experimental import pallas as pl
from jax.experimental.pallas import tpu as pltpu
from jax.sharding import PartitionSpec as P

FEATURES = 64
ITERS = 3
UNROLL = 8
PER_BLOCK = 64
DIAG_SHIFT = 5.0
MESH = pl.DeviceIdType.MESH
F32 = jnp.float32
BF16 = jnp.bfloat16
EVEN = pl.ds(0, 64, stride=2)
ODD = pl.ds(1, 64, stride=2)


def permute(value, matrix, transposed):
    rows = value.shape[0]
    high = value.astype(BF16)
    rest = value - high.astype(F32)
    middle = rest.astype(BF16)
    low = (rest - middle.astype(F32)).astype(BF16)
    parts = jnp.concatenate([high, middle, low], axis=0)
    dims = (((1,), (1 if transposed else 0,)), ((), ()))
    product = lax.dot_general(parts, matrix, dims, preferred_element_type=F32)
    return product[:rows] + product[rows : 2 * rows] + product[2 * rows :]


def swap_pairs(row, swap):
    lane = lax.broadcasted_iota(jnp.int32, row.shape, 1)
    swapped = jnp.where(lane % 2 == 0, pltpu.roll(row, 127, 1), pltpu.roll(row, 1, 1))
    return jnp.where(swap > 0, swapped, row)


def column(row):
    return jnp.broadcast_to(row, (128, 128)).T


def silu_of_half(u):
    return (u + u * jnp.tanh(u)).astype(BF16)


def kernel(
    feat_hbm,
    w1_ref,
    w2_ref,
    w3_ref,
    owner_ref,
    diag_hbm,
    x_hbm,
    y_hbm,
    p_hbm,
    cols_ref,
    xmap_ref,
    yswap_ref,
    adjoint_ref,
    residual_ref,
    feat_ref,
    w1t_ref,
    w2t_ref,
    w3t_ref,
    prod_ref,
    ring_ref,
    plane_out,
    plane_ref,
    index_out,
    index_ref,
    e_ref,
    x_ref,
    y_ref,
    p_ref,
    mp_ref,
    mx_ref,
    vectors,
    vb_ref,
    red_ref,
    acc_ref,
    tmp_ref,
    hx_out,
    hy_out,
    ix_out,
    iy_out,
    hx_in,
    hy_in,
    ix_in,
    iy_in,
    sum_a,
    sum_b,
    local_sem,
    ring_send,
    ring_recv,
    plane_sem,
    index_sem,
    halo_send,
    halo_recv,
    sum_send,
    sum_recv,
):
    i = lax.axis_index("sx")
    j = lax.axis_index("sy")
    y, zh = i // 2, lax.rem(i, 2)
    zl, jl = j // 8, lax.rem(j, 8)
    x, core = jl // 2, lax.rem(j, 2)
    z = zh * 2 + zl

    loads = [
        pltpu.make_async_copy(src, dst, local_sem.at[k])
        for k, (src, dst) in enumerate(
            [(feat_hbm, feat_ref), (diag_hbm, e_ref), (x_hbm, x_ref), (y_hbm, y_ref), (p_hbm, p_ref)]
        )
    ]
    for load in loads:
        load.start()

    def pick(first, second):
        return first * (1 - core) + second * core

    barrier = pltpu.get_barrier_semaphore()

    def greet(k, carry):
        other = (lax.rem(i + k // 16, 8), lax.rem(j + lax.rem(k, 16), 16))
        pl.semaphore_signal(barrier, inc=1, device_id=other, device_id_type=MESH)
        return carry

    lax.fori_loop(1, 128, greet, 0)

    w1t_ref[...] = (w1_ref[...].astype(F32) * 0.5).T.astype(BF16)
    w2t_ref[...] = (w2_ref[...].astype(F32) * 0.5).T.astype(BF16)
    w3t_ref[...] = w3_ref[...].astype(F32).T.astype(BF16)

    kind = lax.rem(x + y + z, 4)
    flat = jnp.where(kind == 0, 1, 0)

    def mod4(value):
        return lax.rem(value + 16, 4)

    def device(dx, dy, dz, dcore):
        return dy * 2 + dz // 2, (lax.rem(dz, 2) * 4 + dx) * 2 + dcore

    def receiver(dx, dy, dz, dcore, part, u):
        if u == 0:
            ry = mod4(dy + part)
            return mod4(-ry - dz), ry, dz
        along = dcore * dx + (1 - dcore) * dy
        moved = mod4(along + part)
        kept = dcore * dy + (1 - dcore) * dx
        return dcore * moved + (1 - dcore) * kept, dcore * kept + (1 - dcore) * moved, mod4(u - moved - kept)

    def summer(s):
        a, b = s // 4, s % 4
        sx, sy, sz = mod4(x + (flat + (1 - flat) * core) * a), 0, 0
        sy = mod4(y + flat * b + (1 - flat) * (1 - core) * a)
        sz = mod4(z + (1 - flat) * b)
        return sx, sy, sz

    def index_place(s):
        return flat * ((4 - s % 4) % 4) * 4 + (1 - flat) * (((4 - s // 4) % 4) * 4 + kind)

    for s in range(16):
        sx, sy, sz = summer(s)
        for q in range(4):
            ex = flat * sx + (1 - flat) * pick(q, sx)
            ey = flat * sy + (1 - flat) * pick(sy, q)
            ez = flat * q + (1 - flat) * sz
            ei, ej = device(ex, ey, ez, 0)
            index_out[s, 2 * q : 2 * q + 2, :] = owner_ref[pl.ds(ei * 16 + ej, 2), :]
    index_ref[index_place(0)] = index_out[0]

    def send_indices():
        for s in range(1, 16):
            pltpu.make_async_remote_copy(
                src_ref=index_out.at[s],
                dst_ref=index_ref.at[index_place(s)],
                send_sem=index_sem.at[0],
                recv_sem=index_sem.at[1],
                device_id=device(*summer(s), core),
                device_id_type=MESH,
            ).start()

    mp_ref[...] = (lax.broadcasted_iota(jnp.int32, (256, 256), 0) == cols_ref[0:1]).astype(F32).astype(BF16)
    mx_ref[...] = (lax.broadcasted_iota(jnp.int32, (128, 128), 0) == xmap_ref[0:1]).astype(F32).astype(BF16)
    yswap = yswap_ref[0:1, 0:1]

    loads[0].wait()

    def routes(h):
        found = []
        for turn in ((1, 3), (2, 0))[h]:
            for own in (0, 1) if turn else (1, 0):
                dcore = own * (1 - core) + (1 - own) * core
                at = (mod4(x + turn * (1 - dcore)), mod4(y + turn * dcore), z, dcore)
                found.append((False, at, ((1 - dcore) * x + dcore * y) * 2 + core))
        for turn in ((1, 3), (2, 0))[h]:
            for own in (0, 1) if turn else (1, 0):
                dcore = own * (1 - core) + (1 - own) * core
                found.append((True, (x, y, mod4(z + turn), dcore), z * 2 + core))
        return found

    def network(part, h):
        blocks = []
        for along_z, at, _ in routes(h):
            for u in (0,) if along_z else (1, 2, 3):
                ri, rj = device(*receiver(*at, part, u), at[3])
                blocks.append(pl.multiple_of((ri * 16 + rj) * 128, 128))
        for half in range(2):
            columns = jnp.concatenate([feat_ref[:, pl.ds(b, 128)] for b in blocks[8 * half : 8 * half + 8]], axis=1)
            hidden = silu_of_half(jnp.dot(w1t_ref[...], columns, preferred_element_type=F32))
            hidden = silu_of_half(jnp.dot(w2t_ref[...], hidden, preferred_element_type=F32))
            output = jnp.dot(w3t_ref[...], hidden, preferred_element_type=F32)
            stress, tangent = output[:64], output[64:]
            tangent = jnp.maximum(tangent, 0.0) + jnp.log(1.0 + jnp.exp(-jnp.abs(tangent)))
            output = jnp.concatenate([stress, tangent * (1.0 / PER_BLOCK)], axis=0).astype(BF16)
            for u in range(8):
                prod_ref[part, 16 * h + 8 * half + u] = output[:, u * 128 : (u + 1) * 128]

        if h == 0:

            @pl.when(part == 0)
            def _():
                pl.semaphore_wait(barrier, 127)

        for r, (along_z, at, slot) in enumerate(routes(h)):
            first = 16 * h + (8 + r if along_z else 3 * r)
            count = 1 if along_z else 3
            source = prod_ref.at[part, pl.ds(first, count)]
            target = ring_ref.at[slot, part, pl.ds(0 if along_z else 1, count)]
            if h == 1 and r in (3, 7):
                target[...] = source[...]
            else:
                pltpu.make_async_remote_copy(
                    src_ref=source,
                    dst_ref=target,
                    send_sem=ring_send.at[int(along_z)],
                    recv_sem=ring_recv.at[int(along_z), slot, part],
                    device_id=device(*at),
                    device_id_type=MESH,
                ).start()

        if h == 0:
            pl.when(part == 0)(send_indices)

    mine = pick(x * 2 + core, y * 2 + core)

    def reduce_rows(part):
        @pl.when(part == 0)
        def _():
            got = index_ref.at[pl.ds(0, 15)]
            pltpu.make_async_copy(got, got, index_sem.at[1]).wait()

        for s in range(1, 8):
            slot = lax.rem(mine + s, 8)
            got = ring_ref.at[slot, part, pl.ds(1, 3)]
            pltpu.make_async_copy(got, got, ring_recv.at[0, slot, part]).wait()
            slot = lax.rem(z * 2 + core + s, 8)
            got = ring_ref.at[slot, part, pl.ds(0, 1)]
            pltpu.make_async_copy(got, got, ring_recv.at[1, slot, part]).wait()
        for u in range(4):
            owners = index_ref[part * 4 + u]
            block = lax.broadcasted_iota(jnp.int32, (256, 128), 0)
            onehot = jnp.concatenate(
                [(block == owners[e : e + 1]).astype(F32).astype(BF16) for e in range(8)], axis=1
            )
            rows = jnp.concatenate([ring_ref[e, part, u] for e in range(8)], axis=1)
            plane_out[part * 4 + u] = lax.dot_general(
                rows, onehot, (((1,), (1,)), ((), ())), preferred_element_type=F32
            ).astype(BF16)
        for u in range(4):
            here = y * 4 + x if u == 0 else pick(y, x) * 4 + z
            self = jnp.logical_and(part == 0, kind == u)

            @pl.when(self)
            def _():
                plane_ref[here] = plane_out[part * 4 + u]

            @pl.when(jnp.logical_not(self))
            def _():
                pltpu.make_async_remote_copy(
                    src_ref=plane_out.at[part * 4 + u],
                    dst_ref=plane_ref.at[here],
                    send_sem=plane_sem.at[0],
                    recv_sem=plane_sem.at[1],
                    device_id=device(*receiver(x, y, z, core, part, u), core),
                    device_id_type=MESH,
                ).start()

    def run_part(part, carry):
        network(part, 0)
        network(part, 1)

        @pl.when(part > 0)
        def _():
            reduce_rows(part - 1)

        return carry

    lax.fori_loop(0, 4, run_part, 0)
    reduce_rows(jnp.int32(3))
    for load in loads[1:]:
        load.wait()
    jac_ref, off_ref, sum_ref, back_ref, *krylov = (vectors.at[k] for k in range(9))
    for k in range(64):
        jac_ref[2 * k : 2 * k + 2, :] = e_ref[k, 2 * k : 2 * k + 2, :]
    pltpu.make_async_copy(plane_ref.at[pl.ds(0, 15)], plane_ref.at[pl.ds(0, 15)], plane_sem.at[1]).wait()
    total = plane_ref[0].astype(F32)
    for t in range(1, 16):
        total = total + plane_ref[t].astype(F32)
    fields = total
    residual_ref[EVEN, :] = fields[:64, :128]
    residual_ref[ODD, :] = fields[:64, 128:]
    off_ref[...] = -2.0 * jac_ref[...]
    jac_ref[EVEN, :] = fields[64:, :128] + DIAG_SHIFT
    jac_ref[ODD, :] = fields[64:, 128:] + DIAG_SHIFT
    jac_ref[...] = jac_ref[...] - off_ref[...]

    x_next, x_prev = (lax.rem(i + 1, 8), j), (lax.rem(i + 7, 8), j)
    y_next, y_prev = (i, lax.rem(j + 1, 16)), (i, lax.rem(j + 15, 16))
    lane = lax.broadcasted_iota(jnp.int32, (128, 128), 1)
    edge_x = jnp.where(i == 7, 0.0, 1.0)
    edge_y = jnp.where(j == 15, 0.0, 1.0)
    start_x = jnp.where(i == 0, 0.0, 1.0)
    start_y = jnp.where(j == 0, 0.0, 1.0)

    def send(src, dst, slot, to):
        copy = pltpu.make_async_remote_copy(
            src_ref=src,
            dst_ref=dst,
            send_sem=halo_send.at[slot],
            recv_sem=halo_recv.at[slot],
            device_id=to,
            device_id_type=MESH,
        )
        copy.start()
        return copy

    def transposed_pass(tiles):
        def body(step, total):
            for u in range(UNROLL):
                k = step * UNROLL + u
                total = total + tiles[k].reshape(16, 8, 128) * vb_ref[k][None]
            return total

        return lax.fori_loop(0, 64 // UNROLL, body, jnp.zeros((16, 8, 128), F32)).reshape(128, 128)

    def forward_pass(tiles, partner):
        partner = partner.reshape(16, 8, 128)

        def body(step, carry):
            for u in range(UNROLL):
                k = step * UNROLL + u
                red_ref[k] += jnp.sum(tiles[k].reshape(16, 8, 128) * partner, axis=0)
            return carry

        lax.fori_loop(0, 64 // UNROLL, body, 0)

    def both_pass(tiles, partner, first):
        partner = partner.reshape(16, 8, 128)

        def body(step, total):
            for u in range(UNROLL):
                k = step * UNROLL + u
                tile = tiles[k].reshape(16, 8, 128)
                forward = jnp.sum(tile * partner, axis=0)
                red_ref[k] = forward if first else red_ref[k] + forward
                total = total + tile * vb_ref[k][None]
            return total

        return lax.fori_loop(0, 64 // UNROLL, body, jnp.zeros((16, 8, 128), F32)).reshape(128, 128)

    index_b = i * 2 + zl

    def sum_begin(rows):
        sum_a[jl] = jnp.concatenate(
            [jnp.sum(row, axis=0, keepdims=True) for row in rows] + [jnp.zeros((8 - len(rows), 128), F32)], axis=0
        )
        for k in range(1, 8):
            pltpu.make_async_remote_copy(
                src_ref=sum_a.at[jl],
                dst_ref=sum_a.at[jl],
                send_sem=sum_send.at[0],
                recv_sem=sum_recv.at[0],
                device_id=(i, zl * 8 + lax.rem(jl + k, 8)),
                device_id_type=MESH,
            ).start()

    def sum_middle():
        pltpu.make_async_copy(sum_a.at[pl.ds(0, 7)], sum_a.at[pl.ds(0, 7)], sum_recv.at[0]).wait()
        sum_b[index_b] = jnp.sum(sum_a[...], axis=0)
        for k in range(1, 16):
            peer = lax.rem(index_b + k, 16)
            pltpu.make_async_remote_copy(
                src_ref=sum_b.at[index_b],
                dst_ref=sum_b.at[index_b],
                send_sem=sum_send.at[1],
                recv_sem=sum_recv.at[1],
                device_id=(peer // 2, lax.rem(peer, 2) * 8 + jl),
                device_id_type=MESH,
            ).start()

    def sum_end():
        pltpu.make_async_copy(sum_b.at[pl.ds(0, 15)], sum_b.at[pl.ds(0, 15)], sum_recv.at[1]).wait()
        total = jnp.sum(jnp.sum(sum_b[...], axis=0), axis=1, keepdims=True)
        return [total[k : k + 1] for k in range(2 * ITERS)]

    sent = []

    def gather_p(even, odd, transposed):
        flat = permute(jnp.concatenate([even, odd], axis=1), mp_ref[...], transposed)
        return flat[:, :128], flat[:, 128:]

    def out_x(it):
        tmp_ref[...] = transposed_pass(x_ref)
        ix_out[it] = permute(tmp_ref[ODD, :], mx_ref[...], True)
        sent.append(send(ix_out.at[it], ix_in.at[it], 4 * it + 2, x_next))
        acc_ref[ODD, :] += tmp_ref[EVEN, :]
        return sent[-1]

    def out_y(it):
        turned = transposed_pass(y_ref)
        iy_out[it] = swap_pairs(turned.T[120:128], yswap)
        sent.append(send(iy_out.at[it], iy_in.at[it], 4 * it + 3, y_next))
        acc_ref[...] += jnp.where(lane == 0, 0.0, pltpu.roll(turned, 1, 1))
        return sent[-1]

    def couple(it, z, moments):
        last = it + 1 == ITERS
        tmp_ref[...] = z
        z_even, z_odd = tmp_ref[EVEN, :], tmp_ref[ODD, :]
        hx_out[it] = z_even
        hx = send(hx_out.at[it], hx_in.at[it], 4 * it, x_prev)
        hy_out[it] = z.T[0:8]
        hy = send(hy_out.at[it], hy_in.at[it], 4 * it + 1, y_prev)
        for q in range(4):
            vb_ref[:, 2 * q, :] = z_even
            vb_ref[:, 2 * q + 1, :] = z_odd
        acc_ref[...] = off_ref[...] * z
        if not last:
            ix, iy = out_x(it), out_y(it)
        acc_ref[...] += both_pass(e_ref, z, True)
        tmp_ref[EVEN, :], tmp_ref[ODD, :] = gather_p(z_even, z_odd, False)
        back_ref[...] = both_pass(p_ref, tmp_ref[...], False)

        def back_p():
            add_even, add_odd = gather_p(back_ref[EVEN, :], back_ref[ODD, :], True)
            acc_ref[EVEN, :] += add_even
            acc_ref[ODD, :] += add_odd

        if not last:
            back_p()
        hx.wait_recv()
        tmp_ref[EVEN, :] = z_odd
        tmp_ref[ODD, :] = permute(hx_in[it], mx_ref[...], False) * edge_x
        forward_pass(x_ref, tmp_ref[...])
        hy.wait_recv()
        beyond = column(swap_pairs(hy_in[it], yswap)[0:1]) * edge_y
        forward_pass(y_ref, jnp.where(lane == 127, beyond, pltpu.roll(z, 127, 1)))
        for a, part in ((0, EVEN), (1, ODD)):
            total = red_ref[:, a, :]
            for q in range(1, 4):
                total = total + red_ref[:, 2 * q + a, :]
            sum_ref[part, :] = total
        acc_ref[...] += sum_ref[...]
        if last:
            sum_begin(moments + [z * (off_ref[...] * z + 2.0 * sum_ref[...])])
            ix, iy = out_x(it), out_y(it)
            sum_middle()
            back_p()
        ix.wait_recv()
        acc_ref[EVEN, :] += ix_in[it] * start_x
        iy.wait_recv()
        acc_ref[...] += jnp.where(lane == 0, column(iy_in[it, 7:8]) * start_y, 0.0)
        sent.extend([hx, hy])
        return acc_ref[...]

    v_refs, r_refs = krylov[:ITERS], [residual_ref] + krylov[ITERS:]
    moments = []
    for it in range(ITERS):
        v_refs[it][...] = r_refs[it][...] / jac_ref[...]
        moments.append(r_refs[it][...] * v_refs[it][...])
        image = couple(it, v_refs[it][...], moments)
        if it + 1 < ITERS:
            r_refs[it + 1][...] = image
            moments.append(image * v_refs[it][...])
    nu = sum_end()

    def ratio(above, below):
        return jnp.where(below == 0.0, 0.0, above / jnp.where(below == 0.0, 1.0, below))

    def form(first, second):
        return sum(a * b * nu[k + m] for k, a in enumerate(first) for m, b in enumerate(second))

    one = jnp.ones((1, 1), F32)
    res, direction, solved = [one], [one], [0.0] * ITERS
    gamma = nu[0]
    for it in range(ITERS):
        moved = [a + b for a, b in zip(direction + [0.0 * one], [0.0 * one] + direction)]
        alpha = ratio(gamma, form(direction, moved))
        solved = [a + alpha * b for a, b in zip(solved, direction)] + solved[len(direction) :]
        res = [a - alpha * b for a, b in zip(res + [0.0 * one], moved)]
        if it + 1 < ITERS:
            gamma_next = form(res, res)
            beta = ratio(gamma_next, gamma)
            direction = [a + beta * b for a, b in zip(res, direction + [0.0 * one])]
            gamma = gamma_next
    adjoint_ref[...] = sum(a * v[...] for a, v in zip(solved, v_refs))
    residual_ref[...] = sum(a * r[...] for a, r in zip(res, r_refs)) + res[ITERS] * image

    for copy in sent:
        copy.wait_send()
    for stage, (buffer, count) in enumerate([(sum_a, 7), (sum_b, 15)]):
        mover = buffer.at[pl.ds(0, count)]
        pltpu.make_async_copy(mover, mover, sum_send.at[stage]).wait()
    out = prod_ref.at[pl.ds(0, 3), pl.ds(0, 28)]
    pltpu.make_async_copy(out, out, ring_send.at[0]).wait()
    out = prod_ref.at[0, pl.ds(0, 28)]
    pltpu.make_async_copy(out, out, ring_send.at[1]).wait()
    pltpu.make_async_copy(plane_ref.at[pl.ds(0, 15)], plane_ref.at[pl.ds(0, 15)], plane_sem.at[0]).wait()
    pltpu.make_async_copy(index_ref.at[pl.ds(0, 15)], index_ref.at[pl.ds(0, 15)], index_sem.at[0]).wait()


def hand_over(adjoint_ref, residual_ref, adjoint_out, residual_out):
    adjoint_out[...] = adjoint_ref[...]
    residual_out[...] = residual_ref[...]


def local(*args):
    (
        quad_features,
        w_first,
        w_second,
        w_third,
        quad_block,
        diag_tiles,
        x_tiles,
        y_tiles,
        p_tiles,
        tile_cols,
        x_map,
        y_map,
    ) = args
    features = quad_features.reshape(16384, FEATURES).T
    tiles = [t.reshape(64, 128, 128) for t in (diag_tiles, x_tiles, y_tiles, p_tiles)]
    owners = quad_block.reshape(128, 128)
    cols = tile_cols.reshape(1, 256)
    xmap = x_map.reshape(1, 128)
    yswap = y_map.reshape(1, 2)
    hbm = pl.BlockSpec(memory_space=pl.ANY)
    vmem = pl.BlockSpec(memory_space=pltpu.VMEM)
    square = pltpu.VMEM((128, 128), F32)
    tile = pltpu.VMEM((64, 128, 128), F32)
    halves = pltpu.VMEM((ITERS, 64, 128), F32)
    strip = pltpu.VMEM((ITERS, 8, 128), F32)
    dma = pltpu.SemaphoreType.DMA
    adjoint, residual = pl.pallas_call(
        kernel,
        out_shape=[jax.ShapeDtypeStruct((128, 128), F32)] * 2,
        in_specs=[hbm, vmem, vmem, vmem, vmem, hbm, hbm, hbm, hbm, vmem, vmem, vmem],
        out_specs=[vmem, vmem],
        scratch_shapes=[
            pltpu.VMEM((FEATURES, 16384), BF16),
            pltpu.VMEM((512, 64), BF16),
            pltpu.VMEM((512, 512), BF16),
            pltpu.VMEM((128, 512), BF16),
            pltpu.VMEM((4, 32, 128, 128), BF16),
            pltpu.VMEM((8, 4, 4, 128, 128), BF16),
            pltpu.VMEM((16, 128, 256), BF16),
            pltpu.VMEM((16, 128, 256), BF16),
            pltpu.VMEM((16, 8, 128), jnp.int32),
            pltpu.VMEM((16, 8, 128), jnp.int32),
            tile,
            tile,
            tile,
            tile,
            pltpu.VMEM((256, 256), BF16),
            pltpu.VMEM((128, 128), BF16),
            pltpu.VMEM((9, 128, 128), F32),
            pltpu.VMEM((64, 8, 128), F32),
            pltpu.VMEM((64, 8, 128), F32),
            square,
            square,
            halves,
            strip,
            halves,
            strip,
            halves,
            strip,
            halves,
            strip,
            pltpu.VMEM((8, 8, 128), F32),
            pltpu.VMEM((16, 8, 128), F32),
            dma((5,)),
            dma((2,)),
            dma((2, 8, 4)),
            dma((2,)),
            dma((2,)),
            dma((4 * ITERS,)),
            dma((4 * ITERS,)),
            dma((2,)),
            dma((2,)),
        ],
        compiler_params=pltpu.CompilerParams(
            collective_id=0, has_side_effects=True, vmem_limit_bytes=56 * 2**20
        ),
    )(features, w_first, w_second, w_third, owners, *tiles, cols, xmap, yswap)
    adjoint, residual = pl.pallas_call(
        hand_over,
        out_shape=[jax.ShapeDtypeStruct((128, 128), F32)] * 2,
        in_specs=[vmem, vmem],
        out_specs=[vmem, vmem],
    )(adjoint, residual)
    return adjoint.reshape(64, 2, 128), residual.reshape(64, 2, 128)


def solution(mesh):
    in_specs = (
        P("sx", "sy", None, None),
        P(),
        P(),
        P(),
        P("sx", "sy", None),
        P(None, None, "sx", "sy"),
        P(None, None, "sx", "sy"),
        P(None, None, "sx", "sy"),
        P(None, None, "sx", "sy"),
        P("sx", "sy", None),
        P("sx", "sy", None),
        P("sx", "sy", None),
    )
    out_specs = (P(None, "sx", "sy"), P(None, "sx", "sy"))
    return jax.shard_map(local, mesh=mesh, in_specs=in_specs, out_specs=out_specs, check_vma=False)
```

```python
import functools

import jax
import jax.numpy as jnp
from jax import lax
from jax.experimental import pallas as pl
from jax.experimental.pallas import tpu as pltpu
from jax.sharding import PartitionSpec as P

FEATURES = 64
ITERS = 3
UNROLL = 8
PER_BLOCK = 64
DIAG_SHIFT = 5.0
MESH = pl.DeviceIdType.MESH
F32 = jnp.float32
BF16 = jnp.bfloat16
EVEN = pl.ds(0, 64, stride=2)
ODD = pl.ds(1, 64, stride=2)


def permute(value, matrix, transposed):
    rows = value.shape[0]
    high = value.astype(BF16)
    rest = value - high.astype(F32)
    middle = rest.astype(BF16)
    low = (rest - middle.astype(F32)).astype(BF16)
    parts = jnp.concatenate([high, middle, low], axis=0)
    dims = (((1,), (1 if transposed else 0,)), ((), ()))
    product = lax.dot_general(parts, matrix, dims, preferred_element_type=F32)
    return product[:rows] + product[rows : 2 * rows] + product[2 * rows :]


def swap_pairs(row, swap):
    lane = lax.broadcasted_iota(jnp.int32, row.shape, 1)
    swapped = jnp.where(lane % 2 == 0, pltpu.roll(row, 127, 1), pltpu.roll(row, 1, 1))
    return jnp.where(swap > 0, swapped, row)


def column(row):
    return jnp.broadcast_to(row, (128, 128)).T


def silu_of_half(u):
    return (u + u * jnp.tanh(u)).astype(BF16)


def kernel(
    feat_hbm,
    w1_ref,
    w2_ref,
    w3_ref,
    owner_ref,
    diag_hbm,
    x_hbm,
    y_hbm,
    p_hbm,
    cols_ref,
    xmap_ref,
    yswap_ref,
    adjoint_ref,
    residual_ref,
    feat_ref,
    w1t_ref,
    w2t_ref,
    w3t_ref,
    prod_ref,
    ring_ref,
    plane_out,
    plane_ref,
    index_out,
    index_ref,
    e_ref,
    x_ref,
    y_ref,
    p_ref,
    mp_ref,
    mx_ref,
    vectors,
    vb_ref,
    red_ref,
    acc_ref,
    tmp_ref,
    hx_out,
    hy_out,
    ix_out,
    iy_out,
    hx_in,
    hy_in,
    ix_in,
    iy_in,
    sum_a,
    sum_b,
    local_sem,
    ring_send,
    ring_recv,
    plane_sem,
    index_sem,
    halo_send,
    halo_recv,
    sum_send,
    sum_recv,
):
    i = lax.axis_index("sx")
    j = lax.axis_index("sy")
    y, zh = i // 2, lax.rem(i, 2)
    zl, jl = j // 8, lax.rem(j, 8)
    x, core = jl // 2, lax.rem(j, 2)

    loads = [
        pltpu.make_async_copy(src, dst, local_sem.at[k])
        for k, (src, dst) in enumerate(
            [(feat_hbm, feat_ref), (diag_hbm, e_ref), (x_hbm, x_ref), (y_hbm, y_ref), (p_hbm, p_ref)]
        )
    ]
    for load in loads:
        load.start()

    def pick(first, second):
        return first * (1 - core) + second * core

    others = [(i, lax.rem(j + k, 16)) for k in range(1, 16)]
    others += [(lax.rem(i + k, 8), j) for k in range(1, 8)]
    others += [(lax.rem(i + k, 8), lax.rem(j + 8, 16)) for k in range(1, 8)]
    others += [(lax.rem(y + k, 4) * 2 + zh, j + 1 - 2 * core) for k in range(1, 4)]
    others += [(y * 2 + 1 - zh, lax.rem(j + 2 * k, 16)) for k in range(1, 8)]
    barrier = pltpu.get_barrier_semaphore()
    for other in others:
        pl.semaphore_signal(barrier, inc=1, device_id=other, device_id_type=MESH)

    w1t_ref[...] = (w1_ref[...].astype(F32) * 0.5).T.astype(BF16)
    w2t_ref[...] = (w2_ref[...].astype(F32) * 0.5).T.astype(BF16)
    w3t_ref[...] = w3_ref[...].astype(F32).T.astype(BF16)

    place_yz, place_xz = i * 2 + zl, zh * 8 + zl * 4 + x
    place = pick(place_yz, place_xz)

    def plane_device(t):
        return pick(t // 2, y * 2 + t // 8), pick(lax.rem(t, 2) * 8 + x * 2, lax.rem(t, 8) * 2 + 1)

    for t in range(16):
        for q in range(4):
            first = pick((t // 2) * 16 + (t % 2) * 8 + q * 2, (q * 2 + t // 8) * 16 + (t % 8) * 2)
            index_out[t, 2 * q : 2 * q + 2, :] = owner_ref[pl.ds(first, 2), :]
    index_ref[place] = index_out[place]

    def send_index(s, carry):
        t = lax.rem(place + s, 16)
        pltpu.make_async_remote_copy(
            src_ref=index_out.at[t],
            dst_ref=index_ref.at[place],
            send_sem=index_sem.at[0],
            recv_sem=index_sem.at[1],
            device_id=plane_device(t),
            device_id_type=MESH,
        ).start()
        return carry

    mp_ref[...] = (lax.broadcasted_iota(jnp.int32, (256, 256), 0) == cols_ref[0:1]).astype(F32).astype(BF16)
    mx_ref[...] = (lax.broadcasted_iota(jnp.int32, (128, 128), 0) == xmap_ref[0:1]).astype(F32).astype(BF16)
    yswap = yswap_ref[0:1, 0:1]

    loads[0].wait()

    def ring_device(q):
        turn = (1, 1, 3, 3, 2, 2, 0, 0)[q]
        dcore = (core, 1 - core, core, 1 - core, core, 1 - core, 1 - core, core)[q]
        return dcore, lax.rem(x + turn * (1 - dcore), 4), lax.rem(y + turn * dcore, 4)

    def network(part):
        for half in range(2):
            columns = []
            for q in range(4 * half, 4 * half + 4):
                dcore, dx, dy = ring_device(q)
                for u in range(2):
                    t = lax.rem((1 - dcore) * place_yz + dcore * place_xz + part * 2 + u, 16)
                    ri = (1 - dcore) * (t // 2) + dcore * (dy * 2 + t // 8)
                    rj = (1 - dcore) * (lax.rem(t, 2) * 8 + dx * 2) + dcore * (lax.rem(t, 8) * 2 + 1)
                    start = pl.multiple_of((ri * 16 + rj) * 128, 128)
                    columns.append(feat_ref[:, pl.ds(start, 128)])
            columns = jnp.concatenate(columns, axis=1)
            hidden = silu_of_half(jnp.dot(w1t_ref[...], columns, preferred_element_type=F32))
            hidden = silu_of_half(jnp.dot(w2t_ref[...], hidden, preferred_element_type=F32))
            output = jnp.dot(w3t_ref[...], hidden, preferred_element_type=F32)
            stress, tangent = output[:64], output[64:]
            tangent = jnp.maximum(tangent, 0.0) + jnp.log(1.0 + jnp.exp(-jnp.abs(tangent)))
            output = jnp.concatenate([stress, tangent * (1.0 / PER_BLOCK)], axis=0).astype(BF16)
            for u in range(8):
                prod_ref[part, 4 * half + u // 2, u % 2] = output[:, u * 128 : (u + 1) * 128]

        @pl.when(part == 0)
        def _():
            pl.semaphore_wait(barrier, len(others))

        for q in range(8):
            dcore, dx, dy = ring_device(q)
            slot = (1 - dcore) * (x * 2 + core) + dcore * (y * 2 + core)
            if q == 7:
                ring_ref[slot, part] = prod_ref[part, q]
            else:
                pltpu.make_async_remote_copy(
                    src_ref=prod_ref.at[part, q],
                    dst_ref=ring_ref.at[slot, part],
                    send_sem=ring_send,
                    recv_sem=ring_recv.at[slot, part],
                    device_id=(dy * 2 + zh, (zl * 4 + dx) * 2 + dcore),
                    device_id_type=MESH,
                ).start()

        @pl.when(part == 0)
        def _():
            lax.fori_loop(1, 16, send_index, 0)

    mine = pick(x * 2 + core, y * 2 + core)

    def reduce_rows(part):
        @pl.when(part == 0)
        def _():
            got = index_ref.at[pl.ds(0, 15)]
            pltpu.make_async_copy(got, got, index_sem.at[1]).wait()

        for s in range(1, 8):
            slot = lax.rem(mine + s, 8)
            got = ring_ref.at[slot, part]
            pltpu.make_async_copy(got, got, ring_recv.at[slot, part]).wait()
        for u in range(2):
            t = lax.rem(place + part * 2 + u, 16)
            owners = index_ref[t]
            block = lax.broadcasted_iota(jnp.int32, (256, 128), 0)
            onehot = jnp.concatenate(
                [(block == owners[e : e + 1]).astype(F32).astype(BF16) for e in range(8)], axis=1
            )
            rows = jnp.concatenate([ring_ref[e, part, u] for e in range(8)], axis=1)
            plane_out[t] = lax.dot_general(
                rows, onehot, (((1,), (1,)), ((), ())), preferred_element_type=F32
            ).astype(BF16)

        def remote(u):
            t = lax.rem(place + part * 2 + u, 16)
            pltpu.make_async_remote_copy(
                src_ref=plane_out.at[t],
                dst_ref=plane_ref.at[place],
                send_sem=plane_sem.at[0],
                recv_sem=plane_sem.at[1],
                device_id=plane_device(t),
                device_id_type=MESH,
            ).start()

        pl.when(part > 0)(functools.partial(remote, 0))
        remote(1)

        @pl.when(part == 0)
        def _():
            plane_ref[place] = plane_out[place]

    def run_part(part, carry):
        network(part)

        @pl.when(part > 1)
        def _():
            reduce_rows(part - 2)

        return carry

    lax.fori_loop(0, 8, run_part, 0)

    def run_rest(part, carry):
        reduce_rows(part)
        return carry

    lax.fori_loop(6, 8, run_rest, 0)
    for load in loads[1:]:
        load.wait()
    jac_ref, off_ref, sum_ref, back_ref, *krylov = (vectors.at[k] for k in range(9))
    for k in range(64):
        jac_ref[2 * k : 2 * k + 2, :] = e_ref[k, 2 * k : 2 * k + 2, :]
    pltpu.make_async_copy(plane_ref.at[pl.ds(0, 15)], plane_ref.at[pl.ds(0, 15)], plane_sem.at[1]).wait()
    total = plane_ref[0].astype(F32)
    for t in range(1, 16):
        total = total + plane_ref[t].astype(F32)
    fields = total
    residual_ref[EVEN, :] = fields[:64, :128]
    residual_ref[ODD, :] = fields[:64, 128:]
    off_ref[...] = -2.0 * jac_ref[...]
    jac_ref[EVEN, :] = fields[64:, :128] + DIAG_SHIFT
    jac_ref[ODD, :] = fields[64:, 128:] + DIAG_SHIFT
    jac_ref[...] = jac_ref[...] - off_ref[...]

    x_next, x_prev = (lax.rem(i + 1, 8), j), (lax.rem(i + 7, 8), j)
    y_next, y_prev = (i, lax.rem(j + 1, 16)), (i, lax.rem(j + 15, 16))
    lane = lax.broadcasted_iota(jnp.int32, (128, 128), 1)
    edge_x = jnp.where(i == 7, 0.0, 1.0)
    edge_y = jnp.where(j == 15, 0.0, 1.0)
    start_x = jnp.where(i == 0, 0.0, 1.0)
    start_y = jnp.where(j == 0, 0.0, 1.0)

    def send(src, dst, slot, to):
        copy = pltpu.make_async_remote_copy(
            src_ref=src,
            dst_ref=dst,
            send_sem=halo_send.at[slot],
            recv_sem=halo_recv.at[slot],
            device_id=to,
            device_id_type=MESH,
        )
        copy.start()
        return copy

    def transposed_pass(tiles):
        def body(step, total):
            for u in range(UNROLL):
                k = step * UNROLL + u
                total = total + tiles[k].reshape(16, 8, 128) * vb_ref[k][None]
            return total

        return lax.fori_loop(0, 64 // UNROLL, body, jnp.zeros((16, 8, 128), F32)).reshape(128, 128)

    def forward_pass(tiles, partner):
        partner = partner.reshape(16, 8, 128)

        def body(step, carry):
            for u in range(UNROLL):
                k = step * UNROLL + u
                red_ref[k] += jnp.sum(tiles[k].reshape(16, 8, 128) * partner, axis=0)
            return carry

        lax.fori_loop(0, 64 // UNROLL, body, 0)

    def both_pass(tiles, partner, first):
        partner = partner.reshape(16, 8, 128)

        def body(step, total):
            for u in range(UNROLL):
                k = step * UNROLL + u
                tile = tiles[k].reshape(16, 8, 128)
                forward = jnp.sum(tile * partner, axis=0)
                red_ref[k] = forward if first else red_ref[k] + forward
                total = total + tile * vb_ref[k][None]
            return total

        return lax.fori_loop(0, 64 // UNROLL, body, jnp.zeros((16, 8, 128), F32)).reshape(128, 128)

    index_b = i * 2 + zl

    def sum_begin(rows):
        sum_a[jl] = jnp.concatenate(
            [jnp.sum(row, axis=0, keepdims=True) for row in rows] + [jnp.zeros((8 - len(rows), 128), F32)], axis=0
        )
        for k in range(1, 8):
            pltpu.make_async_remote_copy(
                src_ref=sum_a.at[jl],
                dst_ref=sum_a.at[jl],
                send_sem=sum_send.at[0],
                recv_sem=sum_recv.at[0],
                device_id=(i, zl * 8 + lax.rem(jl + k, 8)),
                device_id_type=MESH,
            ).start()

    def sum_middle():
        pltpu.make_async_copy(sum_a.at[pl.ds(0, 7)], sum_a.at[pl.ds(0, 7)], sum_recv.at[0]).wait()
        sum_b[index_b] = jnp.sum(sum_a[...], axis=0)
        for k in range(1, 16):
            peer = lax.rem(index_b + k, 16)
            pltpu.make_async_remote_copy(
                src_ref=sum_b.at[index_b],
                dst_ref=sum_b.at[index_b],
                send_sem=sum_send.at[1],
                recv_sem=sum_recv.at[1],
                device_id=(peer // 2, lax.rem(peer, 2) * 8 + jl),
                device_id_type=MESH,
            ).start()

    def sum_end():
        pltpu.make_async_copy(sum_b.at[pl.ds(0, 15)], sum_b.at[pl.ds(0, 15)], sum_recv.at[1]).wait()
        total = jnp.sum(jnp.sum(sum_b[...], axis=0), axis=1, keepdims=True)
        return [total[k : k + 1] for k in range(2 * ITERS)]

    sent = []

    def gather_p(even, odd, transposed):
        flat = permute(jnp.concatenate([even, odd], axis=1), mp_ref[...], transposed)
        return flat[:, :128], flat[:, 128:]

    def out_x(it):
        tmp_ref[...] = transposed_pass(x_ref)
        ix_out[it] = permute(tmp_ref[ODD, :], mx_ref[...], True)
        sent.append(send(ix_out.at[it], ix_in.at[it], 4 * it + 2, x_next))
        acc_ref[ODD, :] += tmp_ref[EVEN, :]
        return sent[-1]

    def out_y(it):
        turned = transposed_pass(y_ref)
        iy_out[it] = swap_pairs(turned.T[120:128], yswap)
        sent.append(send(iy_out.at[it], iy_in.at[it], 4 * it + 3, y_next))
        acc_ref[...] += jnp.where(lane == 0, 0.0, pltpu.roll(turned, 1, 1))
        return sent[-1]

    def couple(it, z, moments):
        last = it + 1 == ITERS
        tmp_ref[...] = z
        z_even, z_odd = tmp_ref[EVEN, :], tmp_ref[ODD, :]
        hx_out[it] = z_even
        hx = send(hx_out.at[it], hx_in.at[it], 4 * it, x_prev)
        hy_out[it] = z.T[0:8]
        hy = send(hy_out.at[it], hy_in.at[it], 4 * it + 1, y_prev)
        for q in range(4):
            vb_ref[:, 2 * q, :] = z_even
            vb_ref[:, 2 * q + 1, :] = z_odd
        acc_ref[...] = off_ref[...] * z
        if not last:
            ix, iy = out_x(it), out_y(it)
        acc_ref[...] += both_pass(e_ref, z, True)
        tmp_ref[EVEN, :], tmp_ref[ODD, :] = gather_p(z_even, z_odd, False)
        back_ref[...] = both_pass(p_ref, tmp_ref[...], False)

        def back_p():
            add_even, add_odd = gather_p(back_ref[EVEN, :], back_ref[ODD, :], True)
            acc_ref[EVEN, :] += add_even
            acc_ref[ODD, :] += add_odd

        if not last:
            back_p()
        hx.wait_recv()
        tmp_ref[EVEN, :] = z_odd
        tmp_ref[ODD, :] = permute(hx_in[it], mx_ref[...], False) * edge_x
        forward_pass(x_ref, tmp_ref[...])
        hy.wait_recv()
        beyond = column(swap_pairs(hy_in[it], yswap)[0:1]) * edge_y
        forward_pass(y_ref, jnp.where(lane == 127, beyond, pltpu.roll(z, 127, 1)))
        for a, part in ((0, EVEN), (1, ODD)):
            total = red_ref[:, a, :]
            for q in range(1, 4):
                total = total + red_ref[:, 2 * q + a, :]
            sum_ref[part, :] = total
        acc_ref[...] += sum_ref[...]
        if last:
            sum_begin(moments + [z * (off_ref[...] * z + 2.0 * sum_ref[...])])
            ix, iy = out_x(it), out_y(it)
            sum_middle()
            back_p()
        ix.wait_recv()
        acc_ref[EVEN, :] += ix_in[it] * start_x
        iy.wait_recv()
        acc_ref[...] += jnp.where(lane == 0, column(iy_in[it, 7:8]) * start_y, 0.0)
        sent.extend([hx, hy])
        return acc_ref[...]

    v_refs, r_refs = krylov[:ITERS], [residual_ref] + krylov[ITERS:]
    moments = []
    for it in range(ITERS):
        v_refs[it][...] = r_refs[it][...] / jac_ref[...]
        moments.append(r_refs[it][...] * v_refs[it][...])
        image = couple(it, v_refs[it][...], moments)
        if it + 1 < ITERS:
            r_refs[it + 1][...] = image
            moments.append(image * v_refs[it][...])
    nu = sum_end()

    def ratio(above, below):
        return jnp.where(below == 0.0, 0.0, above / jnp.where(below == 0.0, 1.0, below))

    def form(first, second):
        return sum(a * b * nu[k + m] for k, a in enumerate(first) for m, b in enumerate(second))

    one = jnp.ones((1, 1), F32)
    res, direction, solved = [one], [one], [0.0] * ITERS
    gamma = nu[0]
    for it in range(ITERS):
        moved = [a + b for a, b in zip(direction + [0.0 * one], [0.0 * one] + direction)]
        alpha = ratio(gamma, form(direction, moved))
        solved = [a + alpha * b for a, b in zip(solved, direction)] + solved[len(direction) :]
        res = [a - alpha * b for a, b in zip(res + [0.0 * one], moved)]
        if it + 1 < ITERS:
            gamma_next = form(res, res)
            beta = ratio(gamma_next, gamma)
            direction = [a + beta * b for a, b in zip(res, direction + [0.0 * one])]
            gamma = gamma_next
    adjoint_ref[...] = sum(a * v[...] for a, v in zip(solved, v_refs))
    residual_ref[...] = sum(a * r[...] for a, r in zip(res, r_refs)) + res[ITERS] * image

    for copy in sent:
        copy.wait_send()
    for stage, (buffer, count) in enumerate([(sum_a, 7), (sum_b, 15)]):
        mover = buffer.at[pl.ds(0, count)]
        pltpu.make_async_copy(mover, mover, sum_send.at[stage]).wait()
    out = prod_ref.at[pl.ds(0, 7)]
    pltpu.make_async_copy(out, out, ring_send).wait()
    pltpu.make_async_copy(plane_ref.at[pl.ds(0, 15)], plane_ref.at[pl.ds(0, 15)], plane_sem.at[0]).wait()
    pltpu.make_async_copy(index_ref.at[pl.ds(0, 15)], index_ref.at[pl.ds(0, 15)], index_sem.at[0]).wait()


def hand_over(adjoint_ref, residual_ref, adjoint_out, residual_out):
    adjoint_out[...] = adjoint_ref[...]
    residual_out[...] = residual_ref[...]


def local(*args):
    (
        quad_features,
        w_first,
        w_second,
        w_third,
        quad_block,
        diag_tiles,
        x_tiles,
        y_tiles,
        p_tiles,
        tile_cols,
        x_map,
        y_map,
    ) = args
    features = quad_features.reshape(16384, FEATURES).T
    tiles = [t.reshape(64, 128, 128) for t in (diag_tiles, x_tiles, y_tiles, p_tiles)]
    owners = quad_block.reshape(128, 128)
    cols = tile_cols.reshape(1, 256)
    xmap = x_map.reshape(1, 128)
    yswap = y_map.reshape(1, 2)
    hbm = pl.BlockSpec(memory_space=pl.ANY)
    vmem = pl.BlockSpec(memory_space=pltpu.VMEM)
    square = pltpu.VMEM((128, 128), F32)
    tile = pltpu.VMEM((64, 128, 128), F32)
    halves = pltpu.VMEM((ITERS, 64, 128), F32)
    strip = pltpu.VMEM((ITERS, 8, 128), F32)
    dma = pltpu.SemaphoreType.DMA
    adjoint, residual = pl.pallas_call(
        kernel,
        out_shape=[jax.ShapeDtypeStruct((128, 128), F32)] * 2,
        in_specs=[hbm, vmem, vmem, vmem, vmem, hbm, hbm, hbm, hbm, vmem, vmem, vmem],
        out_specs=[vmem, vmem],
        scratch_shapes=[
            pltpu.VMEM((FEATURES, 16384), BF16),
            pltpu.VMEM((512, 64), BF16),
            pltpu.VMEM((512, 512), BF16),
            pltpu.VMEM((128, 512), BF16),
            pltpu.VMEM((8, 8, 2, 128, 128), BF16),
            pltpu.VMEM((8, 8, 2, 128, 128), BF16),
            pltpu.VMEM((16, 128, 256), BF16),
            pltpu.VMEM((16, 128, 256), BF16),
            pltpu.VMEM((16, 8, 128), jnp.int32),
            pltpu.VMEM((16, 8, 128), jnp.int32),
            tile,
            tile,
            tile,
            tile,
            pltpu.VMEM((256, 256), BF16),
            pltpu.VMEM((128, 128), BF16),
            pltpu.VMEM((9, 128, 128), F32),
            pltpu.VMEM((64, 8, 128), F32),
            pltpu.VMEM((64, 8, 128), F32),
            square,
            square,
            halves,
            strip,
            halves,
            strip,
            halves,
            strip,
            halves,
            strip,
            pltpu.VMEM((8, 8, 128), F32),
            pltpu.VMEM((16, 8, 128), F32),
            dma((5,)),
            dma,
            dma((8, 8)),
            dma((2,)),
            dma((2,)),
            dma((4 * ITERS,)),
            dma((4 * ITERS,)),
            dma((2,)),
            dma((2,)),
        ],
        compiler_params=pltpu.CompilerParams(
            collective_id=0, has_side_effects=True, vmem_limit_bytes=56 * 2**20
        ),
    )(features, w_first, w_second, w_third, owners, *tiles, cols, xmap, yswap)
    adjoint, residual = pl.pallas_call(
        hand_over,
        out_shape=[jax.ShapeDtypeStruct((128, 128), F32)] * 2,
        in_specs=[vmem, vmem],
        out_specs=[vmem, vmem],
    )(adjoint, residual)
    return adjoint.reshape(64, 2, 128), residual.reshape(64, 2, 128)


def solution(mesh):
    in_specs = (
        P("sx", "sy", None, None),
        P(),
        P(),
        P(),
        P("sx", "sy", None),
        P(None, None, "sx", "sy"),
        P(None, None, "sx", "sy"),
        P(None, None, "sx", "sy"),
        P(None, None, "sx", "sy"),
        P("sx", "sy", None),
        P("sx", "sy", None),
        P("sx", "sy", None),
    )
    out_specs = (P(None, "sx", "sy"), P(None, "sx", "sy"))
    return jax.shard_map(local, mesh=mesh, in_specs=in_specs, out_specs=out_specs, check_vma=False)
```

```python
import functools

import jax
import jax.numpy as jnp
from jax import lax
from jax.experimental import pallas as pl
from jax.experimental.pallas import tpu as pltpu
from jax.sharding import PartitionSpec as P

FEATURES = 64
ITERS = 3
UNROLL = 8
PER_BLOCK = 64
DIAG_SHIFT = 5.0
MESH = pl.DeviceIdType.MESH
F32 = jnp.float32
BF16 = jnp.bfloat16
EVEN = pl.ds(0, 64, stride=2)
ODD = pl.ds(1, 64, stride=2)


def permute(value, matrix, transposed):
    rows = value.shape[0]
    high = value.astype(BF16)
    rest = value - high.astype(F32)
    middle = rest.astype(BF16)
    low = (rest - middle.astype(F32)).astype(BF16)
    parts = jnp.concatenate([high, middle, low], axis=0)
    dims = (((1,), (1 if transposed else 0,)), ((), ()))
    product = lax.dot_general(parts, matrix, dims, preferred_element_type=F32)
    return product[:rows] + product[rows : 2 * rows] + product[2 * rows :]


def swap_pairs(row, swap):
    lane = lax.broadcasted_iota(jnp.int32, row.shape, 1)
    swapped = jnp.where(lane % 2 == 0, pltpu.roll(row, 127, 1), pltpu.roll(row, 1, 1))
    return jnp.where(swap > 0, swapped, row)


def column(row):
    return jnp.broadcast_to(row, (128, 128)).T


def silu_of_half(u):
    return (u + u * jnp.tanh(u)).astype(BF16)


def kernel(
    feat_hbm,
    w1_ref,
    w2_ref,
    w3_ref,
    owner_ref,
    diag_hbm,
    x_hbm,
    y_hbm,
    p_hbm,
    cols_ref,
    xmap_ref,
    yswap_ref,
    adjoint_ref,
    residual_ref,
    feat_ref,
    w1t_ref,
    w2t_ref,
    w3t_ref,
    prod_ref,
    ring_ref,
    plane_out,
    plane_ref,
    index_out,
    index_ref,
    e_ref,
    x_ref,
    y_ref,
    p_ref,
    mp_ref,
    mx_ref,
    vectors,
    vb_ref,
    red_ref,
    acc_ref,
    tmp_ref,
    hx_out,
    hy_out,
    ix_out,
    iy_out,
    hx_in,
    hy_in,
    ix_in,
    iy_in,
    sum_a,
    sum_b,
    local_sem,
    ring_send,
    ring_recv,
    plane_sem,
    index_sem,
    halo_send,
    halo_recv,
    sum_send,
    sum_recv,
):
    i = lax.axis_index("sx")
    j = lax.axis_index("sy")
    y, zh = i // 2, lax.rem(i, 2)
    zl, jl = j // 8, lax.rem(j, 8)
    x, core = jl // 2, lax.rem(j, 2)

    loads = [
        pltpu.make_async_copy(src, dst, local_sem.at[k])
        for k, (src, dst) in enumerate(
            [(feat_hbm, feat_ref), (diag_hbm, e_ref), (x_hbm, x_ref), (y_hbm, y_ref), (p_hbm, p_ref)]
        )
    ]
    for load in loads:
        load.start()

    def pick(first, second):
        return first * (1 - core) + second * core

    others = [(i, lax.rem(j + k, 16)) for k in range(1, 16)]
    others += [(lax.rem(i + k, 8), j) for k in range(1, 8)]
    others += [(lax.rem(i + k, 8), lax.rem(j + 8, 16)) for k in range(1, 8)]
    others += [(lax.rem(y + k, 4) * 2 + zh, j + 1 - 2 * core) for k in range(1, 4)]
    others += [(y * 2 + 1 - zh, lax.rem(j + 2 * k, 16)) for k in range(1, 8)]
    barrier = pltpu.get_barrier_semaphore()
    for other in others:
        pl.semaphore_signal(barrier, inc=1, device_id=other, device_id_type=MESH)

    w1t_ref[...] = (w1_ref[...].astype(F32) * 0.5).T.astype(BF16)
    w2t_ref[...] = (w2_ref[...].astype(F32) * 0.5).T.astype(BF16)
    w3t_ref[...] = w3_ref[...].astype(F32).T.astype(BF16)

    place_yz, place_xz = i * 2 + zl, zh * 8 + zl * 4 + x
    place = pick(place_yz, place_xz)

    def plane_device(t):
        return pick(t // 2, y * 2 + t // 8), pick(lax.rem(t, 2) * 8 + x * 2, lax.rem(t, 8) * 2 + 1)

    for t in range(16):
        for q in range(4):
            first = pick((t // 2) * 16 + (t % 2) * 8 + q * 2, (q * 2 + t // 8) * 16 + (t % 8) * 2)
            index_out[t, 2 * q : 2 * q + 2, :] = owner_ref[pl.ds(first, 2), :]
    index_ref[place] = index_out[place]

    def send_index(s, carry):
        t = lax.rem(place + s, 16)
        pltpu.make_async_remote_copy(
            src_ref=index_out.at[t],
            dst_ref=index_ref.at[place],
            send_sem=index_sem.at[0],
            recv_sem=index_sem.at[1],
            device_id=plane_device(t),
            device_id_type=MESH,
        ).start()
        return carry

    mp_ref[...] = (lax.broadcasted_iota(jnp.int32, (256, 256), 0) == cols_ref[0:1]).astype(F32).astype(BF16)
    mx_ref[...] = (lax.broadcasted_iota(jnp.int32, (128, 128), 0) == xmap_ref[0:1]).astype(F32).astype(BF16)
    yswap = yswap_ref[0:1, 0:1]

    loads[0].wait()

    def ring_device(q):
        turn = (1, 1, 3, 3, 2, 2, 0, 0)[q]
        dcore = (core, 1 - core, core, 1 - core, core, 1 - core, 1 - core, core)[q]
        return dcore, lax.rem(x + turn * (1 - dcore), 4), lax.rem(y + turn * dcore, 4)

    def network(part):
        for half in range(2):
            columns = []
            for q in range(4 * half, 4 * half + 4):
                dcore, dx, dy = ring_device(q)
                for u in range(2):
                    t = lax.rem((1 - dcore) * place_yz + dcore * place_xz + part * 2 + u, 16)
                    ri = (1 - dcore) * (t // 2) + dcore * (dy * 2 + t // 8)
                    rj = (1 - dcore) * (lax.rem(t, 2) * 8 + dx * 2) + dcore * (lax.rem(t, 8) * 2 + 1)
                    start = pl.multiple_of((ri * 16 + rj) * 128, 128)
                    columns.append(feat_ref[:, pl.ds(start, 128)])
            columns = jnp.concatenate(columns, axis=1)
            hidden = silu_of_half(jnp.dot(w1t_ref[...], columns, preferred_element_type=F32))
            hidden = silu_of_half(jnp.dot(w2t_ref[...], hidden, preferred_element_type=F32))
            output = jnp.dot(w3t_ref[...], hidden, preferred_element_type=F32)
            stress, tangent = output[:64], output[64:]
            tangent = jnp.maximum(tangent, 0.0) + jnp.log(1.0 + jnp.exp(-jnp.abs(tangent)))
            output = jnp.concatenate([stress, tangent * (1.0 / PER_BLOCK)], axis=0).astype(BF16)
            for u in range(8):
                prod_ref[part, 4 * half + u // 2, u % 2] = output[:, u * 128 : (u + 1) * 128]

        @pl.when(part == 0)
        def _():
            pl.semaphore_wait(barrier, len(others))

        for q in range(8):
            dcore, dx, dy = ring_device(q)
            slot = (1 - dcore) * (x * 2 + core) + dcore * (y * 2 + core)
            if q == 7:
                ring_ref[slot, part] = prod_ref[part, q]
            else:
                pltpu.make_async_remote_copy(
                    src_ref=prod_ref.at[part, q],
                    dst_ref=ring_ref.at[slot, part],
                    send_sem=ring_send,
                    recv_sem=ring_recv.at[slot, part],
                    device_id=(dy * 2 + zh, (zl * 4 + dx) * 2 + dcore),
                    device_id_type=MESH,
                ).start()

        @pl.when(part == 0)
        def _():
            lax.fori_loop(1, 16, send_index, 0)

    mine = pick(x * 2 + core, y * 2 + core)

    def reduce_rows(part):
        @pl.when(part == 0)
        def _():
            got = index_ref.at[pl.ds(0, 15)]
            pltpu.make_async_copy(got, got, index_sem.at[1]).wait()

        for s in range(1, 8):
            slot = lax.rem(mine + s, 8)
            got = ring_ref.at[slot, part]
            pltpu.make_async_copy(got, got, ring_recv.at[slot, part]).wait()
        for u in range(2):
            t = lax.rem(place + part * 2 + u, 16)
            owners = index_ref[t]
            block = lax.broadcasted_iota(jnp.int32, (256, 128), 0)
            onehot = jnp.concatenate(
                [(block == owners[e : e + 1]).astype(F32).astype(BF16) for e in range(8)], axis=1
            )
            rows = jnp.concatenate([ring_ref[e, part, u] for e in range(8)], axis=1)
            plane_out[t] = lax.dot_general(
                rows, onehot, (((1,), (1,)), ((), ())), preferred_element_type=F32
            ).astype(BF16)

        def remote(u):
            t = lax.rem(place + part * 2 + u, 16)
            pltpu.make_async_remote_copy(
                src_ref=plane_out.at[t],
                dst_ref=plane_ref.at[place],
                send_sem=plane_sem.at[0],
                recv_sem=plane_sem.at[1],
                device_id=plane_device(t),
                device_id_type=MESH,
            ).start()

        pl.when(part > 0)(functools.partial(remote, 0))
        remote(1)

        @pl.when(part == 0)
        def _():
            plane_ref[place] = plane_out[place]

    def run_part(part, carry):
        network(part)

        @pl.when(part > 1)
        def _():
            reduce_rows(part - 2)

        return carry

    lax.fori_loop(0, 8, run_part, 0)

    def run_rest(part, carry):
        reduce_rows(part)
        return carry

    lax.fori_loop(6, 8, run_rest, 0)
    for load in loads[1:]:
        load.wait()
    jac_ref, off_ref, sum_ref, back_ref, *krylov = (vectors.at[k] for k in range(9))
    for k in range(64):
        jac_ref[2 * k : 2 * k + 2, :] = e_ref[k, 2 * k : 2 * k + 2, :]
    pltpu.make_async_copy(plane_ref.at[pl.ds(0, 15)], plane_ref.at[pl.ds(0, 15)], plane_sem.at[1]).wait()
    total = plane_ref[0].astype(F32)
    for t in range(1, 16):
        total = total + plane_ref[t].astype(F32)
    fields = total
    residual_ref[EVEN, :] = fields[:64, :128]
    residual_ref[ODD, :] = fields[:64, 128:]
    off_ref[...] = -2.0 * jac_ref[...]
    jac_ref[EVEN, :] = fields[64:, :128] + DIAG_SHIFT
    jac_ref[ODD, :] = fields[64:, 128:] + DIAG_SHIFT
    jac_ref[...] = jac_ref[...] - off_ref[...]

    x_next, x_prev = (lax.rem(i + 1, 8), j), (lax.rem(i + 7, 8), j)
    y_next, y_prev = (i, lax.rem(j + 1, 16)), (i, lax.rem(j + 15, 16))
    lane = lax.broadcasted_iota(jnp.int32, (128, 128), 1)
    edge_x = jnp.where(i == 7, 0.0, 1.0)
    edge_y = jnp.where(j == 15, 0.0, 1.0)
    start_x = jnp.where(i == 0, 0.0, 1.0)
    start_y = jnp.where(j == 0, 0.0, 1.0)

    def send(src, dst, slot, to):
        copy = pltpu.make_async_remote_copy(
            src_ref=src,
            dst_ref=dst,
            send_sem=halo_send.at[slot],
            recv_sem=halo_recv.at[slot],
            device_id=to,
            device_id_type=MESH,
        )
        copy.start()
        return copy

    def transposed_pass(tiles):
        def body(step, total):
            for u in range(UNROLL):
                k = step * UNROLL + u
                total = total + tiles[k].reshape(16, 8, 128) * vb_ref[k][None]
            return total

        return lax.fori_loop(0, 64 // UNROLL, body, jnp.zeros((16, 8, 128), F32)).reshape(128, 128)

    def forward_pass(tiles, partner, first=False):
        partner = partner.reshape(16, 8, 128)

        def body(step, carry):
            for u in range(UNROLL):
                k = step * UNROLL + u
                forward = jnp.sum(tiles[k].reshape(16, 8, 128) * partner, axis=0)
                red_ref[k] = forward if first else red_ref[k] + forward
            return carry

        lax.fori_loop(0, 64 // UNROLL, body, 0)

    def both_pass(tiles, partner, first):
        partner = partner.reshape(16, 8, 128)

        def body(step, total):
            for u in range(UNROLL):
                k = step * UNROLL + u
                tile = tiles[k].reshape(16, 8, 128)
                forward = jnp.sum(tile * partner, axis=0)
                red_ref[k] = forward if first else red_ref[k] + forward
                total = total + tile * vb_ref[k][None]
            return total

        return lax.fori_loop(0, 64 // UNROLL, body, jnp.zeros((16, 8, 128), F32)).reshape(128, 128)

    index_b = i * 2 + zl

    def sum_begin(rows):
        sum_a[jl] = jnp.concatenate(
            [jnp.sum(row, axis=0, keepdims=True) for row in rows] + [jnp.zeros((8 - len(rows), 128), F32)], axis=0
        )
        for k in range(1, 8):
            pltpu.make_async_remote_copy(
                src_ref=sum_a.at[jl],
                dst_ref=sum_a.at[jl],
                send_sem=sum_send.at[0],
                recv_sem=sum_recv.at[0],
                device_id=(i, zl * 8 + lax.rem(jl + k, 8)),
                device_id_type=MESH,
            ).start()

    def sum_middle():
        pltpu.make_async_copy(sum_a.at[pl.ds(0, 7)], sum_a.at[pl.ds(0, 7)], sum_recv.at[0]).wait()
        sum_b[index_b] = jnp.sum(sum_a[...], axis=0)
        for k in range(1, 16):
            peer = lax.rem(index_b + k, 16)
            pltpu.make_async_remote_copy(
                src_ref=sum_b.at[index_b],
                dst_ref=sum_b.at[index_b],
                send_sem=sum_send.at[1],
                recv_sem=sum_recv.at[1],
                device_id=(peer // 2, lax.rem(peer, 2) * 8 + jl),
                device_id_type=MESH,
            ).start()

    def sum_end():
        pltpu.make_async_copy(sum_b.at[pl.ds(0, 15)], sum_b.at[pl.ds(0, 15)], sum_recv.at[1]).wait()
        total = jnp.sum(jnp.sum(sum_b[...], axis=0), axis=1, keepdims=True)
        return [total[k : k + 1] for k in range(2 * ITERS)]

    sent = []

    def gather_p(even, odd, transposed):
        flat = permute(jnp.concatenate([even, odd], axis=1), mp_ref[...], transposed)
        return flat[:, :128], flat[:, 128:]

    def out_x(it):
        tmp_ref[...] = transposed_pass(x_ref)
        ix_out[it] = permute(tmp_ref[ODD, :], mx_ref[...], True)
        sent.append(send(ix_out.at[it], ix_in.at[it], 4 * it + 2, x_next))
        acc_ref[ODD, :] += tmp_ref[EVEN, :]
        return sent[-1]

    def out_y(it):
        turned = transposed_pass(y_ref)
        iy_out[it] = swap_pairs(turned.T[120:128], yswap)
        sent.append(send(iy_out.at[it], iy_in.at[it], 4 * it + 3, y_next))
        acc_ref[...] += jnp.where(lane == 0, 0.0, pltpu.roll(turned, 1, 1))
        return sent[-1]

    def couple(it, z, moments):
        last = it + 1 == ITERS
        tmp_ref[...] = z
        z_even, z_odd = tmp_ref[EVEN, :], tmp_ref[ODD, :]
        hx_out[it] = z_even
        hx = send(hx_out.at[it], hx_in.at[it], 4 * it, x_prev)
        for q in range(4):
            vb_ref[:, 2 * q, :] = z_even
            vb_ref[:, 2 * q + 1, :] = z_odd
        acc_ref[...] = off_ref[...] * z
        if not last:
            ix = out_x(it)
        hy_out[it] = z.T[0:8]
        hy = send(hy_out.at[it], hy_in.at[it], 4 * it + 1, y_prev)
        if last:
            forward_pass(e_ref, z, True)
        else:
            iy = out_y(it)
            acc_ref[...] += both_pass(e_ref, z, True)
        tmp_ref[EVEN, :], tmp_ref[ODD, :] = gather_p(z_even, z_odd, False)
        if last:
            forward_pass(p_ref, tmp_ref[...])
        else:
            back_ref[...] = both_pass(p_ref, tmp_ref[...], False)

        def back_p():
            add_even, add_odd = gather_p(back_ref[EVEN, :], back_ref[ODD, :], True)
            acc_ref[EVEN, :] += add_even
            acc_ref[ODD, :] += add_odd

        if not last:
            back_p()
        hx.wait_recv()
        tmp_ref[EVEN, :] = z_odd
        tmp_ref[ODD, :] = permute(hx_in[it], mx_ref[...], False) * edge_x
        forward_pass(x_ref, tmp_ref[...])
        hy.wait_recv()
        beyond = column(swap_pairs(hy_in[it], yswap)[0:1]) * edge_y
        forward_pass(y_ref, jnp.where(lane == 127, beyond, pltpu.roll(z, 127, 1)))
        for a, part in ((0, EVEN), (1, ODD)):
            total = red_ref[:, a, :]
            for q in range(1, 4):
                total = total + red_ref[:, 2 * q + a, :]
            sum_ref[part, :] = total
        acc_ref[...] += sum_ref[...]
        if last:
            sum_begin(moments + [z * (off_ref[...] * z + 2.0 * sum_ref[...])])
            ix, iy = out_x(it), out_y(it)
            sum_middle()
            acc_ref[...] += transposed_pass(e_ref)
            back_ref[...] = transposed_pass(p_ref)
            back_p()
        ix.wait_recv()
        acc_ref[EVEN, :] += ix_in[it] * start_x
        iy.wait_recv()
        acc_ref[...] += jnp.where(lane == 0, column(iy_in[it, 7:8]) * start_y, 0.0)
        sent.extend([hx, hy])
        return acc_ref[...]

    v_refs, r_refs = krylov[:ITERS], [residual_ref] + krylov[ITERS:]
    moments = []
    for it in range(ITERS):
        v_refs[it][...] = r_refs[it][...] / jac_ref[...]
        moments.append(r_refs[it][...] * v_refs[it][...])
        image = couple(it, v_refs[it][...], moments)
        if it + 1 < ITERS:
            r_refs[it + 1][...] = image
            moments.append(image * v_refs[it][...])
    nu = sum_end()

    def ratio(above, below):
        return jnp.where(below == 0.0, 0.0, above / jnp.where(below == 0.0, 1.0, below))

    def form(first, second):
        return sum(a * b * nu[k + m] for k, a in enumerate(first) for m, b in enumerate(second))

    one = jnp.ones((1, 1), F32)
    res, direction, solved = [one], [one], [0.0] * ITERS
    gamma = nu[0]
    for it in range(ITERS):
        moved = [a + b for a, b in zip(direction + [0.0 * one], [0.0 * one] + direction)]
        alpha = ratio(gamma, form(direction, moved))
        solved = [a + alpha * b for a, b in zip(solved, direction)] + solved[len(direction) :]
        res = [a - alpha * b for a, b in zip(res + [0.0 * one], moved)]
        if it + 1 < ITERS:
            gamma_next = form(res, res)
            beta = ratio(gamma_next, gamma)
            direction = [a + beta * b for a, b in zip(res, direction + [0.0 * one])]
            gamma = gamma_next
    adjoint_ref[...] = sum(a * v[...] for a, v in zip(solved, v_refs))
    residual_ref[...] = sum(a * r[...] for a, r in zip(res, r_refs)) + res[ITERS] * image

    for copy in sent:
        copy.wait_send()
    for stage, (buffer, count) in enumerate([(sum_a, 7), (sum_b, 15)]):
        mover = buffer.at[pl.ds(0, count)]
        pltpu.make_async_copy(mover, mover, sum_send.at[stage]).wait()
    out = prod_ref.at[pl.ds(0, 7)]
    pltpu.make_async_copy(out, out, ring_send).wait()
    pltpu.make_async_copy(plane_ref.at[pl.ds(0, 15)], plane_ref.at[pl.ds(0, 15)], plane_sem.at[0]).wait()
    pltpu.make_async_copy(index_ref.at[pl.ds(0, 15)], index_ref.at[pl.ds(0, 15)], index_sem.at[0]).wait()


def hand_over(adjoint_ref, residual_ref, adjoint_out, residual_out, sems):
    copies = [
        pltpu.make_async_copy(adjoint_ref, adjoint_out, sems.at[0]),
        pltpu.make_async_copy(residual_ref, residual_out, sems.at[1]),
    ]
    for copy in copies:
        copy.start()
    for copy in copies:
        copy.wait()


def local(*args):
    (
        quad_features,
        w_first,
        w_second,
        w_third,
        quad_block,
        diag_tiles,
        x_tiles,
        y_tiles,
        p_tiles,
        tile_cols,
        x_map,
        y_map,
    ) = args
    features = quad_features.reshape(16384, FEATURES).T
    tiles = [t.reshape(64, 128, 128) for t in (diag_tiles, x_tiles, y_tiles, p_tiles)]
    owners = quad_block.reshape(128, 128)
    cols = tile_cols.reshape(1, 256)
    xmap = x_map.reshape(1, 128)
    yswap = y_map.reshape(1, 2)
    hbm = pl.BlockSpec(memory_space=pl.ANY)
    vmem = pl.BlockSpec(memory_space=pltpu.VMEM)
    square = pltpu.VMEM((128, 128), F32)
    tile = pltpu.VMEM((64, 128, 128), F32)
    halves = pltpu.VMEM((ITERS, 64, 128), F32)
    strip = pltpu.VMEM((ITERS, 8, 128), F32)
    dma = pltpu.SemaphoreType.DMA
    adjoint, residual = pl.pallas_call(
        kernel,
        out_shape=[jax.ShapeDtypeStruct((128, 128), F32)] * 2,
        in_specs=[hbm, vmem, vmem, vmem, vmem, hbm, hbm, hbm, hbm, vmem, vmem, vmem],
        out_specs=[vmem, vmem],
        scratch_shapes=[
            pltpu.VMEM((FEATURES, 16384), BF16),
            pltpu.VMEM((512, 64), BF16),
            pltpu.VMEM((512, 512), BF16),
            pltpu.VMEM((128, 512), BF16),
            pltpu.VMEM((8, 8, 2, 128, 128), BF16),
            pltpu.VMEM((8, 8, 2, 128, 128), BF16),
            pltpu.VMEM((16, 128, 256), BF16),
            pltpu.VMEM((16, 128, 256), BF16),
            pltpu.VMEM((16, 8, 128), jnp.int32),
            pltpu.VMEM((16, 8, 128), jnp.int32),
            tile,
            tile,
            tile,
            tile,
            pltpu.VMEM((256, 256), BF16),
            pltpu.VMEM((128, 128), BF16),
            pltpu.VMEM((9, 128, 128), F32),
            pltpu.VMEM((64, 8, 128), F32),
            pltpu.VMEM((64, 8, 128), F32),
            square,
            square,
            halves,
            strip,
            halves,
            strip,
            halves,
            strip,
            halves,
            strip,
            pltpu.VMEM((8, 8, 128), F32),
            pltpu.VMEM((16, 8, 128), F32),
            dma((5,)),
            dma,
            dma((8, 8)),
            dma((2,)),
            dma((2,)),
            dma((4 * ITERS,)),
            dma((4 * ITERS,)),
            dma((2,)),
            dma((2,)),
        ],
        compiler_params=pltpu.CompilerParams(
            collective_id=0, has_side_effects=True, vmem_limit_bytes=56 * 2**20
        ),
    )(features, w_first, w_second, w_third, owners, *tiles, cols, xmap, yswap)
    adjoint, residual = pl.pallas_call(
        hand_over,
        out_shape=[jax.ShapeDtypeStruct((128, 128), F32)] * 2,
        in_specs=[hbm, hbm],
        out_specs=[hbm, hbm],
        scratch_shapes=[dma((2,))],
    )(adjoint, residual)
    return adjoint.reshape(64, 2, 128), residual.reshape(64, 2, 128)


def solution(mesh):
    in_specs = (
        P("sx", "sy", None, None),
        P(),
        P(),
        P(),
        P("sx", "sy", None),
        P(None, None, "sx", "sy"),
        P(None, None, "sx", "sy"),
        P(None, None, "sx", "sy"),
        P(None, None, "sx", "sy"),
        P("sx", "sy", None),
        P("sx", "sy", None),
        P("sx", "sy", None),
    )
    out_specs = (P(None, "sx", "sy"), P(None, "sx", "sy"))
    return jax.shard_map(local, mesh=mesh, in_specs=in_specs, out_specs=out_specs, check_vma=False)
```

```python
import functools

import jax
import jax.numpy as jnp
from jax import lax
from jax.experimental import pallas as pl
from jax.experimental.pallas import tpu as pltpu
from jax.sharding import PartitionSpec as P

FEATURES = 64
ITERS = 3
UNROLL = 16
PER_BLOCK = 64
DIAG_SHIFT = 5.0
MESH = pl.DeviceIdType.MESH
F32 = jnp.float32
BF16 = jnp.bfloat16
EVEN = pl.ds(0, 64, stride=2)
ODD = pl.ds(1, 64, stride=2)


def permute(value, matrix, transposed):
    rows = value.shape[0]
    high = value.astype(BF16)
    rest = value - high.astype(F32)
    middle = rest.astype(BF16)
    low = (rest - middle.astype(F32)).astype(BF16)
    parts = jnp.concatenate([high, middle, low], axis=0)
    dims = (((1,), (1 if transposed else 0,)), ((), ()))
    product = lax.dot_general(parts, matrix, dims, preferred_element_type=F32)
    return product[:rows] + product[rows : 2 * rows] + product[2 * rows :]


def swap_pairs(row, swap):
    lane = lax.broadcasted_iota(jnp.int32, row.shape, 1)
    swapped = jnp.where(lane % 2 == 0, pltpu.roll(row, 127, 1), pltpu.roll(row, 1, 1))
    return jnp.where(swap > 0, swapped, row)


def column(row):
    return jnp.broadcast_to(row, (128, 128)).T


def silu_of_half(u):
    return (u + u * jnp.tanh(u)).astype(BF16)


def kernel(
    feat_hbm,
    w1_ref,
    w2_ref,
    w3_ref,
    owner_ref,
    diag_hbm,
    x_hbm,
    y_hbm,
    p_hbm,
    cols_ref,
    xmap_ref,
    yswap_ref,
    adjoint_ref,
    residual_ref,
    feat_ref,
    w1t_ref,
    w2t_ref,
    w3t_ref,
    prod_ref,
    ring_ref,
    plane_out,
    plane_ref,
    index_out,
    index_ref,
    e_ref,
    x_ref,
    y_ref,
    p_ref,
    mp_ref,
    mx_ref,
    vectors,
    vb_ref,
    red_ref,
    acc_ref,
    tmp_ref,
    hx_out,
    hy_out,
    ix_out,
    iy_out,
    hx_in,
    hy_in,
    ix_in,
    iy_in,
    sum_a,
    sum_b,
    local_sem,
    ring_send,
    ring_recv,
    plane_sem,
    index_sem,
    halo_send,
    halo_recv,
    sum_send,
    sum_recv,
):
    i = lax.axis_index("sx")
    j = lax.axis_index("sy")
    y, zh = i // 2, lax.rem(i, 2)
    zl, jl = j // 8, lax.rem(j, 8)
    x, core = jl // 2, lax.rem(j, 2)

    loads = [
        pltpu.make_async_copy(src, dst, local_sem.at[k])
        for k, (src, dst) in enumerate(
            [(feat_hbm, feat_ref), (diag_hbm, e_ref), (x_hbm, x_ref), (y_hbm, y_ref), (p_hbm, p_ref)]
        )
    ]
    for load in loads:
        load.start()

    def pick(first, second):
        return first * (1 - core) + second * core

    others = [(i, lax.rem(j + k, 16)) for k in range(1, 16)]
    others += [(lax.rem(i + k, 8), j) for k in range(1, 8)]
    others += [(lax.rem(i + k, 8), lax.rem(j + 8, 16)) for k in range(1, 8)]
    others += [(lax.rem(y + k, 4) * 2 + zh, j + 1 - 2 * core) for k in range(1, 4)]
    others += [(y * 2 + 1 - zh, lax.rem(j + 2 * k, 16)) for k in range(1, 8)]
    barrier = pltpu.get_barrier_semaphore()
    for other in others:
        pl.semaphore_signal(barrier, inc=1, device_id=other, device_id_type=MESH)

    w1t_ref[...] = (w1_ref[...].astype(F32) * 0.5).T.astype(BF16)
    w2t_ref[...] = (w2_ref[...].astype(F32) * 0.5).T.astype(BF16)
    w3t_ref[...] = w3_ref[...].astype(F32).T.astype(BF16)

    place_yz, place_xz = i * 2 + zl, zh * 8 + zl * 4 + x
    place = pick(place_yz, place_xz)

    def plane_device(t):
        return pick(t // 2, y * 2 + t // 8), pick(lax.rem(t, 2) * 8 + x * 2, lax.rem(t, 8) * 2 + 1)

    for t in range(16):
        for q in range(4):
            first = pick((t // 2) * 16 + (t % 2) * 8 + q * 2, (q * 2 + t // 8) * 16 + (t % 8) * 2)
            index_out[t, 2 * q : 2 * q + 2, :] = owner_ref[pl.ds(first, 2), :]
    index_ref[place] = index_out[place]

    def send_index(s, carry):
        t = lax.rem(place + s, 16)
        pltpu.make_async_remote_copy(
            src_ref=index_out.at[t],
            dst_ref=index_ref.at[place],
            send_sem=index_sem.at[0],
            recv_sem=index_sem.at[1],
            device_id=plane_device(t),
            device_id_type=MESH,
        ).start()
        return carry

    mp_ref[...] = (lax.broadcasted_iota(jnp.int32, (256, 256), 0) == cols_ref[0:1]).astype(F32).astype(BF16)
    mx_ref[...] = (lax.broadcasted_iota(jnp.int32, (128, 128), 0) == xmap_ref[0:1]).astype(F32).astype(BF16)
    yswap = yswap_ref[0:1, 0:1]

    loads[0].wait()

    def ring_device(q):
        turn = (1, 1, 3, 3, 2, 2, 0, 0)[q]
        dcore = (core, 1 - core, core, 1 - core, core, 1 - core, 1 - core, core)[q]
        return dcore, lax.rem(x + turn * (1 - dcore), 4), lax.rem(y + turn * dcore, 4)

    def network(part):
        for half in range(2):
            columns = []
            for q in range(4 * half, 4 * half + 4):
                dcore, dx, dy = ring_device(q)
                for u in range(2):
                    t = lax.rem((1 - dcore) * place_yz + dcore * place_xz + part * 2 + u, 16)
                    ri = (1 - dcore) * (t // 2) + dcore * (dy * 2 + t // 8)
                    rj = (1 - dcore) * (lax.rem(t, 2) * 8 + dx * 2) + dcore * (lax.rem(t, 8) * 2 + 1)
                    start = pl.multiple_of((ri * 16 + rj) * 128, 128)
                    columns.append(feat_ref[:, pl.ds(start, 128)])
            columns = jnp.concatenate(columns, axis=1)
            hidden = silu_of_half(jnp.dot(w1t_ref[...], columns, preferred_element_type=F32))
            hidden = silu_of_half(jnp.dot(w2t_ref[...], hidden, preferred_element_type=F32))
            output = jnp.dot(w3t_ref[...], hidden, preferred_element_type=F32)
            stress, tangent = output[:64], output[64:]
            tangent = jnp.maximum(tangent, 0.0) + jnp.log(1.0 + jnp.exp(-jnp.abs(tangent)))
            output = jnp.concatenate([stress, tangent * (1.0 / PER_BLOCK)], axis=0).astype(BF16)
            for u in range(8):
                prod_ref[part, 4 * half + u // 2, u % 2] = output[:, u * 128 : (u + 1) * 128]

        @pl.when(part == 0)
        def _():
            pl.semaphore_wait(barrier, len(others))

        for q in range(8):
            dcore, dx, dy = ring_device(q)
            slot = (1 - dcore) * (x * 2 + core) + dcore * (y * 2 + core)
            if q == 7:
                ring_ref[slot, part] = prod_ref[part, q]
            else:
                pltpu.make_async_remote_copy(
                    src_ref=prod_ref.at[part, q],
                    dst_ref=ring_ref.at[slot, part],
                    send_sem=ring_send,
                    recv_sem=ring_recv.at[slot, part],
                    device_id=(dy * 2 + zh, (zl * 4 + dx) * 2 + dcore),
                    device_id_type=MESH,
                ).start()

        @pl.when(part == 0)
        def _():
            lax.fori_loop(1, 16, send_index, 0)

    mine = pick(x * 2 + core, y * 2 + core)

    def reduce_rows(part):
        @pl.when(part == 0)
        def _():
            got = index_ref.at[pl.ds(0, 15)]
            pltpu.make_async_copy(got, got, index_sem.at[1]).wait()

        for s in range(1, 8):
            slot = lax.rem(mine + s, 8)
            got = ring_ref.at[slot, part]
            pltpu.make_async_copy(got, got, ring_recv.at[slot, part]).wait()
        for u in range(2):
            t = lax.rem(place + part * 2 + u, 16)
            owners = index_ref[t]
            block = lax.broadcasted_iota(jnp.int32, (256, 128), 0)
            onehot = jnp.concatenate(
                [(block == owners[e : e + 1]).astype(F32).astype(BF16) for e in range(8)], axis=1
            )
            rows = jnp.concatenate([ring_ref[e, part, u] for e in range(8)], axis=1)
            plane_out[t] = lax.dot_general(
                rows, onehot, (((1,), (1,)), ((), ())), preferred_element_type=F32
            ).astype(BF16)

        def remote(u):
            t = lax.rem(place + part * 2 + u, 16)
            pltpu.make_async_remote_copy(
                src_ref=plane_out.at[t],
                dst_ref=plane_ref.at[place],
                send_sem=plane_sem.at[0],
                recv_sem=plane_sem.at[1],
                device_id=plane_device(t),
                device_id_type=MESH,
            ).start()

        pl.when(part > 0)(functools.partial(remote, 0))
        remote(1)

        @pl.when(part == 0)
        def _():
            plane_ref[place] = plane_out[place]

    def run_part(part, carry):
        network(part)

        @pl.when(part > 1)
        def _():
            reduce_rows(part - 2)

        return carry

    lax.fori_loop(0, 8, run_part, 0)

    def run_rest(part, carry):
        reduce_rows(part)
        return carry

    lax.fori_loop(6, 8, run_rest, 0)
    for load in loads[1:]:
        load.wait()
    jac_ref, off_ref, sum_ref, back_ref, *krylov = (vectors.at[k] for k in range(9))
    for k in range(64):
        jac_ref[2 * k : 2 * k + 2, :] = e_ref[k, 2 * k : 2 * k + 2, :]
    pltpu.make_async_copy(plane_ref.at[pl.ds(0, 15)], plane_ref.at[pl.ds(0, 15)], plane_sem.at[1]).wait()
    total = plane_ref[0].astype(F32)
    for t in range(1, 16):
        total = total + plane_ref[t].astype(F32)
    fields = total
    residual_ref[EVEN, :] = fields[:64, :128]
    residual_ref[ODD, :] = fields[:64, 128:]
    off_ref[...] = -2.0 * jac_ref[...]
    jac_ref[EVEN, :] = fields[64:, :128] + DIAG_SHIFT
    jac_ref[ODD, :] = fields[64:, 128:] + DIAG_SHIFT
    jac_ref[...] = jac_ref[...] - off_ref[...]

    x_next, x_prev = (lax.rem(i + 1, 8), j), (lax.rem(i + 7, 8), j)
    y_next, y_prev = (i, lax.rem(j + 1, 16)), (i, lax.rem(j + 15, 16))
    lane = lax.broadcasted_iota(jnp.int32, (128, 128), 1)
    edge_x = jnp.where(i == 7, 0.0, 1.0)
    edge_y = jnp.where(j == 15, 0.0, 1.0)
    start_x = jnp.where(i == 0, 0.0, 1.0)
    start_y = jnp.where(j == 0, 0.0, 1.0)

    def send(src, dst, slot, to):
        copy = pltpu.make_async_remote_copy(
            src_ref=src,
            dst_ref=dst,
            send_sem=halo_send.at[slot],
            recv_sem=halo_recv.at[slot],
            device_id=to,
            device_id_type=MESH,
        )
        copy.start()
        return copy

    def transposed_pass(tiles):
        def body(step, total):
            for u in range(UNROLL):
                k = step * UNROLL + u
                total = total + tiles[k].reshape(16, 8, 128) * vb_ref[k][None]
            return total

        return lax.fori_loop(0, 64 // UNROLL, body, jnp.zeros((16, 8, 128), F32)).reshape(128, 128)

    def forward_pass(tiles, partner, first=False):
        partner = partner.reshape(16, 8, 128)

        def body(step, carry):
            for u in range(UNROLL):
                k = step * UNROLL + u
                forward = jnp.sum(tiles[k].reshape(16, 8, 128) * partner, axis=0)
                red_ref[k] = forward if first else red_ref[k] + forward
            return carry

        lax.fori_loop(0, 64 // UNROLL, body, 0)

    def both_pass(tiles, partner, first):
        partner = partner.reshape(16, 8, 128)

        def body(step, total):
            for u in range(UNROLL):
                k = step * UNROLL + u
                tile = tiles[k].reshape(16, 8, 128)
                forward = jnp.sum(tile * partner, axis=0)
                red_ref[k] = forward if first else red_ref[k] + forward
                total = total + tile * vb_ref[k][None]
            return total

        return lax.fori_loop(0, 64 // UNROLL, body, jnp.zeros((16, 8, 128), F32)).reshape(128, 128)

    index_b = i * 2 + zl

    def sum_begin(rows):
        sum_a[jl] = jnp.concatenate(
            [jnp.sum(row, axis=0, keepdims=True) for row in rows] + [jnp.zeros((8 - len(rows), 128), F32)], axis=0
        )
        for k in range(1, 8):
            pltpu.make_async_remote_copy(
                src_ref=sum_a.at[jl],
                dst_ref=sum_a.at[jl],
                send_sem=sum_send.at[0],
                recv_sem=sum_recv.at[0],
                device_id=(i, zl * 8 + lax.rem(jl + k, 8)),
                device_id_type=MESH,
            ).start()

    def sum_middle():
        pltpu.make_async_copy(sum_a.at[pl.ds(0, 7)], sum_a.at[pl.ds(0, 7)], sum_recv.at[0]).wait()
        sum_b[index_b] = jnp.sum(sum_a[...], axis=0)
        for k in range(1, 16):
            peer = lax.rem(index_b + k, 16)
            pltpu.make_async_remote_copy(
                src_ref=sum_b.at[index_b],
                dst_ref=sum_b.at[index_b],
                send_sem=sum_send.at[1],
                recv_sem=sum_recv.at[1],
                device_id=(peer // 2, lax.rem(peer, 2) * 8 + jl),
                device_id_type=MESH,
            ).start()

    def sum_end():
        pltpu.make_async_copy(sum_b.at[pl.ds(0, 15)], sum_b.at[pl.ds(0, 15)], sum_recv.at[1]).wait()
        total = jnp.sum(jnp.sum(sum_b[...], axis=0), axis=1, keepdims=True)
        return [total[k : k + 1] for k in range(2 * ITERS)]

    sent = []

    def gather_p(even, odd, transposed):
        flat = permute(jnp.concatenate([even, odd], axis=1), mp_ref[...], transposed)
        return flat[:, :128], flat[:, 128:]

    def out_x(it):
        tmp_ref[...] = transposed_pass(x_ref)
        ix_out[it] = permute(tmp_ref[ODD, :], mx_ref[...], True)
        sent.append(send(ix_out.at[it], ix_in.at[it], 4 * it + 2, x_next))
        acc_ref[ODD, :] += tmp_ref[EVEN, :]
        return sent[-1]

    def out_y(it):
        turned = transposed_pass(y_ref)
        iy_out[it] = swap_pairs(turned.T[120:128], yswap)
        sent.append(send(iy_out.at[it], iy_in.at[it], 4 * it + 3, y_next))
        acc_ref[...] += jnp.where(lane == 0, 0.0, pltpu.roll(turned, 1, 1))
        return sent[-1]

    def couple(it, z, moments):
        last = it + 1 == ITERS
        tmp_ref[...] = z
        z_even, z_odd = tmp_ref[EVEN, :], tmp_ref[ODD, :]
        hx_out[it] = z_even
        hx = send(hx_out.at[it], hx_in.at[it], 4 * it, x_prev)
        for q in range(4):
            vb_ref[:, 2 * q, :] = z_even
            vb_ref[:, 2 * q + 1, :] = z_odd
        acc_ref[...] = off_ref[...] * z
        if not last:
            ix = out_x(it)
        hy_out[it] = z.T[0:8]
        hy = send(hy_out.at[it], hy_in.at[it], 4 * it + 1, y_prev)
        if last:
            forward_pass(e_ref, z, True)
        else:
            iy = out_y(it)
            acc_ref[...] += both_pass(e_ref, z, True)
        tmp_ref[EVEN, :], tmp_ref[ODD, :] = gather_p(z_even, z_odd, False)
        if last:
            forward_pass(p_ref, tmp_ref[...])
        else:
            back_ref[...] = both_pass(p_ref, tmp_ref[...], False)

        def back_p():
            add_even, add_odd = gather_p(back_ref[EVEN, :], back_ref[ODD, :], True)
            acc_ref[EVEN, :] += add_even
            acc_ref[ODD, :] += add_odd

        if not last:
            back_p()
        hx.wait_recv()
        tmp_ref[EVEN, :] = z_odd
        tmp_ref[ODD, :] = permute(hx_in[it], mx_ref[...], False) * edge_x
        forward_pass(x_ref, tmp_ref[...])
        hy.wait_recv()
        beyond = column(swap_pairs(hy_in[it], yswap)[0:1]) * edge_y
        forward_pass(y_ref, jnp.where(lane == 127, beyond, pltpu.roll(z, 127, 1)))
        for a, part in ((0, EVEN), (1, ODD)):
            total = red_ref[:, a, :]
            for q in range(1, 4):
                total = total + red_ref[:, 2 * q + a, :]
            sum_ref[part, :] = total
        acc_ref[...] += sum_ref[...]
        if last:
            sum_begin(moments + [z * (off_ref[...] * z + 2.0 * sum_ref[...])])
            ix, iy = out_x(it), out_y(it)
            sum_middle()
            acc_ref[...] += transposed_pass(e_ref)
            back_ref[...] = transposed_pass(p_ref)
            back_p()
        ix.wait_recv()
        acc_ref[EVEN, :] += ix_in[it] * start_x
        iy.wait_recv()
        acc_ref[...] += jnp.where(lane == 0, column(iy_in[it, 7:8]) * start_y, 0.0)
        sent.extend([hx, hy])
        return acc_ref[...]

    v_refs, r_refs = krylov[:ITERS], [residual_ref] + krylov[ITERS:]
    moments = []
    for it in range(ITERS):
        v_refs[it][...] = r_refs[it][...] / jac_ref[...]
        moments.append(r_refs[it][...] * v_refs[it][...])
        image = couple(it, v_refs[it][...], moments)
        if it + 1 < ITERS:
            r_refs[it + 1][...] = image
            moments.append(image * v_refs[it][...])
    nu = sum_end()

    def ratio(above, below):
        return jnp.where(below == 0.0, 0.0, above / jnp.where(below == 0.0, 1.0, below))

    def form(first, second):
        return sum(a * b * nu[k + m] for k, a in enumerate(first) for m, b in enumerate(second))

    one = jnp.ones((1, 1), F32)
    res, direction, solved = [one], [one], [0.0] * ITERS
    gamma = nu[0]
    for it in range(ITERS):
        moved = [a + b for a, b in zip(direction + [0.0 * one], [0.0 * one] + direction)]
        alpha = ratio(gamma, form(direction, moved))
        solved = [a + alpha * b for a, b in zip(solved, direction)] + solved[len(direction) :]
        res = [a - alpha * b for a, b in zip(res + [0.0 * one], moved)]
        if it + 1 < ITERS:
            gamma_next = form(res, res)
            beta = ratio(gamma_next, gamma)
            direction = [a + beta * b for a, b in zip(res, direction + [0.0 * one])]
            gamma = gamma_next
    adjoint_ref[...] = sum(a * v[...] for a, v in zip(solved, v_refs))
    residual_ref[...] = sum(a * r[...] for a, r in zip(res, r_refs)) + res[ITERS] * image

    for copy in sent:
        copy.wait_send()
    for stage, (buffer, count) in enumerate([(sum_a, 7), (sum_b, 15)]):
        mover = buffer.at[pl.ds(0, count)]
        pltpu.make_async_copy(mover, mover, sum_send.at[stage]).wait()
    out = prod_ref.at[pl.ds(0, 7)]
    pltpu.make_async_copy(out, out, ring_send).wait()
    pltpu.make_async_copy(plane_ref.at[pl.ds(0, 15)], plane_ref.at[pl.ds(0, 15)], plane_sem.at[0]).wait()
    pltpu.make_async_copy(index_ref.at[pl.ds(0, 15)], index_ref.at[pl.ds(0, 15)], index_sem.at[0]).wait()


def hand_over(adjoint_ref, residual_ref, adjoint_out, residual_out):
    adjoint_out[...] = adjoint_ref[...]
    residual_out[...] = residual_ref[...]


def local(*args):
    (
        quad_features,
        w_first,
        w_second,
        w_third,
        quad_block,
        diag_tiles,
        x_tiles,
        y_tiles,
        p_tiles,
        tile_cols,
        x_map,
        y_map,
    ) = args
    features = quad_features.reshape(16384, FEATURES).T
    tiles = [t.reshape(64, 128, 128) for t in (diag_tiles, x_tiles, y_tiles, p_tiles)]
    owners = quad_block.reshape(128, 128)
    cols = tile_cols.reshape(1, 256)
    xmap = x_map.reshape(1, 128)
    yswap = y_map.reshape(1, 2)
    hbm = pl.BlockSpec(memory_space=pl.ANY)
    vmem = pl.BlockSpec(memory_space=pltpu.VMEM)
    square = pltpu.VMEM((128, 128), F32)
    tile = pltpu.VMEM((64, 128, 128), F32)
    halves = pltpu.VMEM((ITERS, 64, 128), F32)
    strip = pltpu.VMEM((ITERS, 8, 128), F32)
    dma = pltpu.SemaphoreType.DMA
    adjoint, residual = pl.pallas_call(
        kernel,
        out_shape=[jax.ShapeDtypeStruct((128, 128), F32)] * 2,
        in_specs=[hbm, vmem, vmem, vmem, vmem, hbm, hbm, hbm, hbm, vmem, vmem, vmem],
        out_specs=[vmem, vmem],
        scratch_shapes=[
            pltpu.VMEM((FEATURES, 16384), BF16),
            pltpu.VMEM((512, 64), BF16),
            pltpu.VMEM((512, 512), BF16),
            pltpu.VMEM((128, 512), BF16),
            pltpu.VMEM((8, 8, 2, 128, 128), BF16),
            pltpu.VMEM((8, 8, 2, 128, 128), BF16),
            pltpu.VMEM((16, 128, 256), BF16),
            pltpu.VMEM((16, 128, 256), BF16),
            pltpu.VMEM((16, 8, 128), jnp.int32),
            pltpu.VMEM((16, 8, 128), jnp.int32),
            tile,
            tile,
            tile,
            tile,
            pltpu.VMEM((256, 256), BF16),
            pltpu.VMEM((128, 128), BF16),
            pltpu.VMEM((9, 128, 128), F32),
            pltpu.VMEM((64, 8, 128), F32),
            pltpu.VMEM((64, 8, 128), F32),
            square,
            square,
            halves,
            strip,
            halves,
            strip,
            halves,
            strip,
            halves,
            strip,
            pltpu.VMEM((8, 8, 128), F32),
            pltpu.VMEM((16, 8, 128), F32),
            dma((5,)),
            dma,
            dma((8, 8)),
            dma((2,)),
            dma((2,)),
            dma((4 * ITERS,)),
            dma((4 * ITERS,)),
            dma((2,)),
            dma((2,)),
        ],
        compiler_params=pltpu.CompilerParams(
            collective_id=0, has_side_effects=True, vmem_limit_bytes=56 * 2**20
        ),
    )(features, w_first, w_second, w_third, owners, *tiles, cols, xmap, yswap)
    adjoint, residual = pl.pallas_call(
        hand_over,
        out_shape=[jax.ShapeDtypeStruct((128, 128), F32)] * 2,
        in_specs=[vmem, vmem],
        out_specs=[vmem, vmem],
    )(adjoint, residual)
    return adjoint.reshape(64, 2, 128), residual.reshape(64, 2, 128)


def solution(mesh):
    in_specs = (
        P("sx", "sy", None, None),
        P(),
        P(),
        P(),
        P("sx", "sy", None),
        P(None, None, "sx", "sy"),
        P(None, None, "sx", "sy"),
        P(None, None, "sx", "sy"),
        P(None, None, "sx", "sy"),
        P("sx", "sy", None),
        P("sx", "sy", None),
        P("sx", "sy", None),
    )
    out_specs = (P(None, "sx", "sy"), P(None, "sx", "sy"))
    return jax.shard_map(local, mesh=mesh, in_specs=in_specs, out_specs=out_specs, check_vma=False)
```
